512 devices in a mesh: tm: 32 (over z_lo, x, core), rows: 16 (over y, z_hi).
Axes of the slice: x: 4, y: 4, z: 16 (z_hi: 4, z_lo: 4; z = z_hi * 4 + z_lo), core: 2. Of those that a mesh axis runs over, the one named last changes fastest.
Arguments:
- starts: float32 [32, 2, 128, 8192], P('tm', None, 'rows'), may hold values from -6 to 6
- conductivity: float32 [128, 8192], P('rows'), may hold values from 0.03 to 0.12
Outputs:
- new_ends: float32 [32, 2, 128, 8192], P('tm', None, 'rows')
- coarse_next: float32 [32, 2, 16, 1024], P('tm')
The draws below stay inside these ranges and needn't reach their ends.
All inputs are finite; a program needn't handle non-finite values.
Results may differ from the reference program's by a relative error of at most 0.0001.
Values sent between devices are 32-bit elements; how exact they have to be, the bound alone decides.
No kernel may reach another device: no remote copies, remote signals or barrier semaphores. Data moves between devices by JAX's collectives and lax.ppermute only.
A program may use at most 64 MiB of HBM per device.

```python
import math
import jax
import jax.numpy as jnp
from jax import lax

NY = 8192
FINE = 8
COARSE = 2
COARSEN = 8
SLICES = 32
NX = 128


def shard_levels(own_key, extent, cuts, least, largest):
    def one(dim, shards_of):
        draws = jax.random.uniform(jax.random.fold_in(jax.random.fold_in(own_key, 6), dim), (shards_of,), jnp.float32, least / len(cuts), largest / len(cuts))
        return jnp.repeat(jnp.exp(draws), extent[dim] // shards_of).reshape((-1,) + (1,) * (len(extent) - dim - 1))

    factor_of = one(*cuts[0])
    for cut in cuts[1:]:
        factor_of = factor_of * one(*cut)
    return factor_of


def scatter_about(key, dims, deviation, limit, pieces=(), kind=jnp.bfloat16):
    values = jax.random.normal(key, dims, jnp.float32) * deviation
    if len(pieces) > 0:
        values = shard_levels(key, dims, pieces, -0.22, 0.18) * values
    return jnp.clip(values, min=-limit, max=limit).astype(kind)


def setup_inputs(seed: int = 0) -> dict:
    arg_keys = jax.random.split(jax.random.key(seed), 3)
    return {
        "starts": scatter_about(arg_keys[0], (SLICES, 2, NX, NY), 1.0, 6.0, ((0, 32), (2, 16)), jnp.float32),
        "conductivity": jnp.clip(jnp.exp(math.log(0.12) - 1.3862944 * jax.random.uniform(arg_keys[1], (NX, NY), jnp.float32) ** shard_levels(arg_keys[1], (NX, NY), ((0, 16),), -0.2, 0.2)), 0.03, 0.12),
    }


EXCHANGE = 0.05
TRACER_DIFF = 0.5


def advance(extended, kappa_ext, step_len, spacing_sq):
    centre = extended[:, 1:-1]
    kappa_mid = kappa_ext[1:-1]
    upper = 0.5 * (kappa_mid + kappa_ext[2:])
    lower = 0.5 * (kappa_mid + kappa_ext[:-2])
    right_face = 0.5 * (kappa_mid + jnp.roll(kappa_mid, -1, 1))
    left_face = 0.5 * (kappa_mid + jnp.roll(kappa_mid, 1, 1))
    spread = (upper * (extended[:, 2:] - centre) + lower * (extended[:, :-2] - centre)
              + right_face * (jnp.roll(centre, -1, 2) - centre)
              + left_face * (jnp.roll(centre, 1, 2) - centre)) / spacing_sq
    transfer = EXCHANGE * (centre[1] - centre[0])
    heat = centre[0] + step_len * (spread[0] + transfer)
    tracer = centre[1] + step_len * (TRACER_DIFF * spread[1] - transfer)
    return jnp.stack([heat, tracer])


def pad_fields(values):
    return jnp.pad(values, ((0, 0), (1, 1), (0, 0)))


def pad_kappa(values):
    return jnp.pad(values, ((1, 1), (0, 0)))


def restrict(values):
    lead = values.shape[:-2]
    nrow = values.shape[-2]
    ncol = values.shape[-1]
    blocks = values.reshape(lead + (nrow // COARSEN, COARSEN, ncol // COARSEN, COARSEN))
    return jnp.mean(blocks, axis=(-3, -1))


def prolong(values):
    return jnp.repeat(jnp.repeat(values, COARSEN, -2), COARSEN, -1)


def coarse_prop(coarse, kappa_coarse):
    kappa_ext = pad_kappa(kappa_coarse)
    for substep in range(COARSE):
        coarse = advance(pad_fields(coarse), kappa_ext, FINE / COARSE, float(COARSEN * COARSEN))
    return coarse


def fine_prop(fields, conductivity):
    kappa_ext = pad_kappa(conductivity)
    for substep in range(FINE):
        fields = advance(pad_fields(fields), kappa_ext, 1.0, 1.0)
    return fields


def reference(starts, conductivity):
    kappa_coarse = restrict(conductivity)

    def per_slice(start):
        fine_end = fine_prop(start, conductivity)
        old = coarse_prop(restrict(start), kappa_coarse)
        return fine_end - prolong(old)

    defects = lax.map(per_slice, starts)
    coarse_defects = restrict(defects)

    def link(coarse, defect):
        advanced = coarse_prop(coarse, kappa_coarse)
        following = advanced + defect
        return following, (advanced, following)

    last, outputs = lax.scan(link, restrict(starts[0]), coarse_defects)
    advanced_all, following_all = outputs
    return prolong(advanced_all) + defects, following_all
```

```python
import jax
import jax.numpy as jnp
from jax import lax
from jax.experimental import pallas as pl
from jax.experimental.pallas import tpu as pltpu
from jax.sharding import Mesh, PartitionSpec as P

FINE = 8
COARSE = 2
COARSEN = 8
EXCHANGE = 0.05
TRACER_DIFF = 0.5

ZL, XC, CORE = 4, 4, 2
GROUP = XC * CORE
ROWS = 16
NY = 8192
CHUNKS = 8
WIDE = NY // CHUNKS
TILES = WIDE // 128
HALO = 8
BATCH = 4
FIRST = 1
FRAME = 28
F32 = jnp.float32
SPLIT, TIES = False, (4, 4)
VMEM_LIMIT = 48 * 1024 * 1024


def lanes():
    return lax.broadcasted_iota(jnp.int32, (8, 128), 1)


def right_of(tiles, lane):
    first = pltpu.roll(tiles[0], 127, 1)
    return tiles[1:] + [jnp.where(lane == 127, pltpu.roll(first, 7, 0), first)]


def left_of(tiles, lane):
    last = pltpu.roll(tiles[-1], 1, 1)
    return [jnp.where(lane == 0, pltpu.roll(last, 1, 0), last)] + tiles[:-1]


def tile_at(r, t):
    return pl.ds(pl.multiple_of(r * 64 + t * 8, 8), 8)


def row_of(ref, r):
    return [ref[tile_at(r, t), :] for t in range(TILES)]


def permutation(inverse):
    a = lax.broadcasted_iota(jnp.int32, (WIDE, WIDE), 1 if inverse else 0)
    b = lax.broadcasted_iota(jnp.int32, (WIDE, WIDE), 0 if inverse else 1)
    return jnp.where((a % 8) * 128 + a // 8 == b, 1.0, 0.0).astype(jnp.bfloat16)


def permuted(x, order):
    total = None
    for _ in range(3):
        part = x.astype(jnp.bfloat16)
        x = x - part.astype(F32)
        moved = jnp.dot(part, order, preferred_element_type=F32)
        total = moved if total is None else total + moved
    return total


def to_frame(piece, out, order):
    x = jnp.concatenate([piece(slice(c * WIDE, (c + 1) * WIDE)) for c in range(CHUNKS)], axis=0)
    x = permuted(x, order)
    for c in range(CHUNKS):
        for t in range(TILES):
            out[pl.ds(t * 8 + c, 8, stride=64), :] = x[8 * c:8 * c + 8, 128 * t:128 * (t + 1)]


def sum_rows(ref, first):
    total = row_of(ref, first)
    for r in range(1, 8):
        total = [a + b for a, b in zip(total, row_of(ref, first + r))]
    return total


def restrict_sum(total):
    while len(total) > 1:
        total = [a + b for a, b in zip(total[::2], total[1::2])]
    return total[0] * (1.0 / (COARSEN * COARSEN))


def faces(k_ref, kr_ref, kd_ref):
    lane = lanes()

    def batch(i, _):
        k = row_of(k_ref, i * BATCH)
        for n in range(BATCH):
            r = i * BATCH + n
            below = row_of(k_ref, jnp.minimum(r + 1, FRAME - 1))
            right = right_of(k, lane)
            for t in range(TILES):
                kr_ref[tile_at(r, t), :] = 0.5 * (k[t] + right[t])
                kd_ref[tile_at(r, t), :] = 0.5 * (k[t] + below[t])
            k = below
        return 0

    lax.fori_loop(0, FRAME // BATCH, batch, 0)


def sweep(old, new, kr_ref, kd_ref, low, count):
    lane = lanes()

    def batch(i, _):
        base = low + i * BATCH
        flux = [None, None]
        for f in range(2):
            above = jnp.maximum(base - 1, 0)
            v, below, face = row_of(old[f], above), row_of(old[f], base), row_of(kd_ref, above)
            flux[f] = [face[t] * (below[t] - v[t]) for t in range(TILES)]
        for n in range(BATCH):
            r = base + n
            kr, kd = row_of(kr_ref, r), row_of(kd_ref, r)
            now, spread = [], []
            for f, ref in enumerate(old):
                v, below = row_of(ref, r), row_of(ref, r + 1)
                right = right_of(v, lane)
                side = [kr[t] * (right[t] - v[t]) for t in range(TILES)]
                left = left_of(side, lane)
                down = [kd[t] * (below[t] - v[t]) for t in range(TILES)]
                spread.append([(side[t] - left[t]) + (down[t] - flux[f][t]) for t in range(TILES)])
                flux[f] = down
                now.append(v)
            for t in range(TILES):
                move = EXCHANGE * (now[1][t] - now[0][t])
                new[0][tile_at(r, t), :] = now[0][t] + (spread[0][t] + move)
                new[1][tile_at(r, t), :] = now[1][t] + (TRACER_DIFF * spread[1][t] - move)
        return 0

    lax.fori_loop(0, (count + BATCH - 1) // BATCH, batch, 0)


def clear_outside(row, fields):
    @pl.when(row == 0)
    def _():
        for ref in fields:
            ref[pl.ds((FIRST + 7) * 64, 64), :] = jnp.zeros((64, 128), F32)

    @pl.when(row == ROWS - 1)
    def _():
        for ref in fields:
            ref[pl.ds((FIRST + 16) * 64, 64), :] = jnp.zeros((64, 128), F32)


def clear_margins(fields):
    for ref in fields:
        ref[0:FIRST * 64, :] = jnp.zeros((FIRST * 64, 128), F32)
        ref[(FIRST + 24) * 64:FRAME * 64, :] = jnp.zeros(((FRAME - FIRST - 24) * 64, 128), F32)


def conductivity_kernel(core_ref, k_ref, kf_ref, half_ref, kc_ref):
    to_frame(lambda c: k_ref[:, c], kf_ref, permutation(False))
    half_ref[...] = kf_ref[pl.ds(pl.multiple_of(core_ref[0] * 256, 256), 256), :]
    kc_ref[...] = restrict_sum(sum_rows(kf_ref, 0))


def two_fields(refs):
    return (refs[0].at[0], refs[0].at[1]) if len(refs) == 1 else refs


def start_kernel(u_ref, *refs):
    order = permutation(False)
    rs_ref = refs[-1]
    for f, ref in enumerate(two_fields(refs[:-1])):
        to_frame(lambda c, f=f: u_ref[f, :, c], ref, order)
        rs_ref[f] = restrict_sum(sum_rows(ref, 0))


def window_start(j):
    return (j - 1) // 2


def early_kernel(rs_ref, kc_ref, out_ref):
    out_ref[...] = jnp.zeros_like(out_ref)
    for j in range(ROWS):
        for t in range(2):
            c = (window_start(j) + t) % CHUNKS
            for k in range(2):
                out_ref[j, pl.ds(t * 4 + k, 1), :] = rs_ref[k, pl.ds(c, 1), :]
            out_ref[j, pl.ds(t * 4 + 2, 1), :] = kc_ref[pl.ds(c, 1), :]


def conductivity_frame(core, k_ref, mine_ref, other_ref, k, kr, kd):
    clear_margins((k,))
    k[(FIRST + HALO) * 64:(FIRST + 2 * HALO) * 64, :] = k_ref[...]
    for part, half in ((mine_ref, core), (other_ref, 1 - core)):
        for side in range(2):
            at = (FIRST + 2 * HALO * side) * 64 + half * 256
            k[pl.ds(pl.multiple_of(at, 64), 256), :] = part[side]
    faces(k, kr, kd)


def steps(one, other, row, kr, kd, low, count, grow):
    def pair(i, _):
        for n, (old, new) in enumerate(((one, other), (other, one))):
            done = 2 * i + n
            sweep(old, new, kr, kd, FIRST + low - grow * done, count + 2 * grow * done)
            clear_outside(row, new)
        return 0

    lax.fori_loop(0, FINE // 2, pair, 0)


def local_kernel(place_ref, *refs):
    out_ref, h, t, h2, t2, k, kr, kd, mix = refs[-9:]
    k_ref, mine_ref, other_ref = refs[-12:-9]
    own = two_fields(refs[:-12])
    conductivity_frame(place_ref[1], k_ref, mine_ref, other_ref, k, kr, kd)
    for ref in (h, t, h2, t2):
        ref[...] = jnp.zeros_like(ref)
    for part, ref in zip(own, (h, t)):
        ref[(FIRST + HALO) * 64:(FIRST + 2 * HALO) * 64, :] = part[...]
    steps((h, t), (h2, t2), place_ref[0], kr, kd, HALO - 1, HALO + 2, 1)
    mix[...] = jnp.zeros_like(mix)
    for b in range(3):
        for f, ref in enumerate((h, t)):
            mix[pl.ds(2 * b + f, 8, stride=8), :] = restrict_sum(sum_rows(ref, FIRST + HALO * b))
    for j in range(ROWS):
        for s in range(2):
            c = (window_start(j) + s) % CHUNKS
            out_ref[j, 8 * s:8 * (s + 1), :] = mix[8 * c:8 * (c + 1), :]


def window_kernel(got_ref, early_ref, w_ref, rf_ref, kc_ref):
    first = lax.broadcasted_iota(jnp.int32, (16, 128), 0)
    for s in range(2):
        kc_ref[16 * s:16 * (s + 1), :] = early_ref[pl.ds(4 * s + 2, 16, stride=8), :]
        for f in range(2):
            up = got_ref[pl.ds(8 * s + f, 16, stride=16), :]
            own = got_ref[pl.ds(8 * s + 2 + f, 16, stride=16), :]
            down = got_ref[pl.ds(8 * s + 4 + f, 16, stride=16), :]
            total = own + jnp.where(first == 0, 0.0, pltpu.roll(down, 1, 0))
            total = total + jnp.where(first == 15, 0.0, pltpu.roll(up, 15, 0))
            at = slice(32 * s + 16 * f, 32 * s + 16 * f + 16)
            rf_ref[at, :] = total
            w = total - early_ref[pl.ds(4 * s + f, 16, stride=8), :]
            for m in range(GROUP):
                w_ref[m, at, :] = w


def field(ref, f):
    return jnp.concatenate([ref[16 * f:16 * f + 16, :], ref[32 + 16 * f:48 + 16 * f, :]], axis=1)


def put(ref, f, x):
    ref[16 * f:16 * f + 16, :] = x[:, :128]
    ref[32 + 16 * f:48 + 16 * f, :] = x[:, 128:]


def coarse_coefficients(kc_ref):
    k = jnp.concatenate([kc_ref[0:16, :], kc_ref[16:32, :]], axis=1)
    width = k.shape[1]
    row = lax.broadcasted_iota(jnp.int32, k.shape, 0)
    scale = 0.5 * (FINE / COARSE) / (COARSEN * COARSEN)
    up = scale * (k + jnp.where(row == 0, 0.0, pltpu.roll(k, 1, 0)))
    down = scale * (k + jnp.where(row == 15, 0.0, pltpu.roll(k, 15, 0)))
    right = scale * (k + pltpu.roll(k, width - 1, 1))
    left = scale * (k + pltpu.roll(k, 1, 1))
    total = up + down + right + left
    keep = 1.0 - EXCHANGE * FINE / COARSE
    return (jnp.where(row == 0, 0.0, up), jnp.where(row == 15, 0.0, down), right, left,
            keep - total, keep - TRACER_DIFF * total)


def coarse_apply(e, coefficients):
    up, down, right, left, mid_h, mid_t = coefficients
    width = up.shape[1]
    trade = EXCHANGE * FINE / COARSE

    def around(v):
        return (up * pltpu.roll(v, 1, 0) + down * pltpu.roll(v, 15, 0)) + (
            right * pltpu.roll(v, width - 1, 1) + left * pltpu.roll(v, 1, 1))

    h, t = e
    for _ in range(COARSE):
        h, t = (around(h) + (mid_h * h + trade * t),
                TRACER_DIFF * around(t) + (mid_t * t + trade * h))
    return h, t


def group_kernel(place_ref, got_ref, kc_ref, sum_ref, own_ref):
    place = place_ref[0]
    coefficients = coarse_coefficients(kc_ref)
    shape = coefficients[0].shape
    zero = jnp.zeros(shape, F32)
    put(own_ref, 0, zero)
    put(own_ref, 1, zero)

    def link(m, e):
        @pl.when(m == place)
        def _():
            put(own_ref, 0, e[0])
            put(own_ref, 1, e[1])
        nxt = coarse_apply(e, coefficients)
        w = got_ref.at[m]
        return nxt[0] + field(w, 0), nxt[1] + field(w, 1)

    e = lax.fori_loop(0, GROUP, link, (zero, zero))
    for g in range(ZL):
        put(sum_ref.at[g], 0, e[0])
        put(sum_ref.at[g], 1, e[1])


def close_kernel(place_ref, got_ref, kc_ref, own_ref, rf_ref, out_ref):
    place, group, block = place_ref[0], place_ref[1], place_ref[2]
    coefficients = coarse_coefficients(kc_ref)
    zero = jnp.zeros(coefficients[0].shape, F32)

    def repeat(count, e):
        return lax.fori_loop(0, count, lambda _, x: coarse_apply(x, coefficients), e)

    def link(g, e):
        e = repeat(jnp.where(g == 0, 0, GROUP), e)
        got = got_ref.at[g]
        return e[0] + field(got, 0), e[1] + field(got, 1)

    e = lax.fori_loop(0, group, link, (zero, zero))
    e = repeat(jnp.where(group == 0, 0, place), e)
    e = coarse_apply((e[0] + field(own_ref, 0), e[1] + field(own_ref, 1)), coefficients)
    h, t = e[0] + field(rf_ref, 0), e[1] + field(rf_ref, 1)
    odd = block % 2 == 1
    lane = lax.broadcasted_iota(jnp.int32, (16, 128), 1)
    middle = [jnp.where(odd, pltpu.roll(x[:, :128], 64, 1), x[:, 128:]) for x in (h, t)]
    both = jnp.where(lane < 64, middle[0], pltpu.roll(middle[1], 64, 1))
    for j in range(ROWS):
        out_ref[j] = both


def finish_kernel(place_ref, *refs):
    ends_ref, next_ref, h, t, h2, t2, k, kr, kd = refs[-9:]
    k_ref, mine_ref, other_ref, got_ref = refs[-13:-9]
    fields = refs[:-13]
    each = len(fields) // 3
    above, own, below = (two_fields(fields[each * n:each * (n + 1)]) for n in range(3))
    lane = lanes()
    row = place_ref[0]
    conductivity_frame(place_ref[1], k_ref, mine_ref, other_ref, k, kr, kd)
    clear_margins((h, t, h2, t2))
    for ref, parts in zip((h, t), zip(above, own, below)):
        for n, part in enumerate(parts):
            at = (FIRST + n * HALO) * 64
            ref[at:at + HALO * 64, :] = part[...]
    steps((h, t), (h2, t2), row, kr, kd, 1, 3 * HALO - 2, -1)

    wide = lax.broadcasted_iota(jnp.int32, (16, 128), 1)
    for q in range(CHUNKS):
        even, odd = got_ref[32 * q:32 * q + 16, :], got_ref[32 * q + 16:32 * q + 32, :]
        cols = slice(128 * q, 128 * (q + 1))
        next_ref[0, :, cols] = jnp.where(wide < 64, even, pltpu.roll(odd, 64, 1))
        next_ref[1, :, cols] = jnp.where(wide < 64, pltpu.roll(even, 64, 1), odd)
    even = got_ref[pl.ds(row, 8, stride=32), :]
    odd = got_ref[pl.ds(row + 16, 8, stride=32), :]
    mine = (jnp.where(lane < 64, even, pltpu.roll(odd, 64, 1)), jnp.where(lane < 64, pltpu.roll(even, 64, 1), odd))
    back = permutation(True)
    for f, ref in enumerate((h, t)):
        change = mine[f] - restrict_sum(sum_rows(ref, FIRST + HALO))
        for r in range(FIRST + HALO, FIRST + 2 * HALO):
            for s in range(TILES):
                ref[tile_at(r, s), :] = ref[tile_at(r, s), :] + change
        x = jnp.concatenate([
            jnp.concatenate([ref[pl.ds((FIRST + HALO) * 64 + s * 8 + c, 8, stride=64), :] for s in range(TILES)], axis=1)
            for c in range(CHUNKS)], axis=0)
        x = permuted(x, back)
        for c in range(CHUNKS):
            ends_ref[f, :, c * WIDE:(c + 1) * WIDE] = x[8 * c:8 * c + 8, :]


def call(kernel, outs, scratch, args, scalars=0, name=None, us=1):
    vmem = pl.BlockSpec(memory_space=pltpu.VMEM)
    specs = [pl.BlockSpec(memory_space=pltpu.SMEM)] * scalars + [vmem] * (len(args) - scalars)
    shapes = [jax.ShapeDtypeStruct(s, F32) for s in outs]
    single = len(outs) == 1
    return pl.pallas_call(
        kernel,
        out_shape=shapes[0] if single else shapes,
        in_specs=specs,
        out_specs=vmem if single else [vmem] * len(outs),
        scratch_shapes=[pltpu.VMEM(s, F32) for s in scratch],
        compiler_params=pltpu.CompilerParams(vmem_limit_bytes=VMEM_LIMIT),
        name=name,
        cost_estimate=pl.CostEstimate(flops=0, bytes_accessed=us * 3690000, transcendentals=0),
    )(*args)


def body(starts, conductivity):
    rows_axes, tm_axes = ("y", "z_hi"), ("z_lo", "x", "core")
    u = starts[0]
    row = lax.axis_index(rows_axes).astype(jnp.int32)
    group = lax.axis_index("z_lo").astype(jnp.int32)
    place = lax.axis_index(("x", "core")).astype(jnp.int32)
    core = lax.axis_index("core").astype(jnp.int32)
    here = jnp.stack([row, core])
    places = jnp.stack([place, group, row])

    def from_above(x):
        return lax.ppermute(x, rows_axes, [(i, i + 1) for i in range(ROWS - 1)])

    def from_below(x):
        return lax.ppermute(x, rows_axes, [(i + 1, i) for i in range(ROWS - 1)])

    kf, half, kc = call(conductivity_kernel, [(512, 128), (256, 128), (8, 128)], [], (core[None], conductivity), 1,
                        name="frame_conductivity", us=2)
    k_up, k_down = from_above(half), from_below(half)
    if SPLIT:
        *fields, rs = call(start_kernel, [(512, 128), (512, 128), (2, 8, 128)], [], (u,), name="frame_starts", us=3)
    else:
        *fields, rs = call(start_kernel, [(2, 512, 128), (2, 8, 128)], [], (u,), name="frame_starts", us=3)
    above, below = [from_above(x) for x in fields], [from_below(x) for x in fields]
    slices = ZL * GROUP
    rs_next = lax.ppermute(rs, tm_axes, [(i + 1, i) for i in range(slices - 1)])
    early = call(early_kernel, [(ROWS, 8, 128)], [], (rs_next, kc), name="early_windows")
    early, k_up, k_down = lax.optimization_barrier((early, k_up, k_down))
    mine = jnp.stack([k_up, k_down])
    other = lax.ppermute(mine, "core", [(0, 1), (1, 0)])
    early = lax.all_to_all(early, rows_axes, 0, 0)

    def hold(x, n):
        tied = lax.optimization_barrier((x, above[n], below[n]))
        above[n], below[n] = tied[1:]
        return tied[0]

    frame = (FRAME * 64, 128)
    parts = call(local_kernel, [(ROWS, 16, 128)], [frame] * 7 + [(64, 128)],
                 (here, *fields, kf, mine, other), 1, name="own_contributions", us=7)
    for n in range(len(fields)):
        if TIES[n] == 0:
            parts = hold(parts, n)
    parts = lax.all_to_all(parts, rows_axes, 0, 0)
    for n in range(len(fields)):
        if TIES[n] == 1:
            parts = hold(parts, n)
    w, rf, kcw = call(window_kernel, [(GROUP, 64, 128), (64, 128), (32, 128)], [],
                      (parts.reshape(ROWS * 16, 128), early.reshape(ROWS * 8, 128)), name="windows")
    for n in range(len(fields)):
        if TIES[n] == 2:
            w = hold(w, n)
    w = lax.all_to_all(w, ("x", "core"), 0, 0)
    for n in range(len(fields)):
        if TIES[n] == 3:
            w = hold(w, n)
    sums, own = call(group_kernel, [(ZL, 64, 128), (64, 128)], [], (places, w, kcw), 1, name="chain_in_group", us=3)
    for n in range(len(fields)):
        if TIES[n] == 4:
            sums = hold(sums, n)
    sums = lax.all_to_all(sums, "z_lo", 0, 0)
    for n in range(len(fields)):
        if TIES[n] == 5:
            sums = hold(sums, n)
    after = call(close_kernel, [(ROWS, 16, 128)], [], (places, sums, kcw, own, rf), 1, name="chain_over_groups", us=4)
    after = lax.all_to_all(after, rows_axes, 0, 0)
    ends, following = call(finish_kernel, [(2, HALO, NY), (2, ROWS, NY // COARSEN)], [frame] * 7,
                           (here, *above, *fields, *below, kf, mine, other, after.reshape(ROWS * 16, 128)), 1,
                           name="fine_and_ends", us=9)
    return ends[None], following[None]


def solution(mesh):
    fine_mesh = Mesh(mesh.devices.reshape(ZL, XC, CORE, 4, 4), ("z_lo", "x", "core", "y", "z_hi"))
    tm, rows = ("z_lo", "x", "core"), ("y", "z_hi")
    in_specs = (P(tm, None, rows, None), P(rows, None))
    out_specs = (P(tm, None, rows, None), P(tm, None, None, None))
    return jax.shard_map(body, mesh=fine_mesh, in_specs=in_specs, out_specs=out_specs, check_vma=False)
```

```python
import jax
import jax.numpy as jnp
from jax import lax
from jax.experimental import pallas as pl
from jax.experimental.pallas import tpu as pltpu
from jax.sharding import Mesh, PartitionSpec as P

FINE = 8
COARSE = 2
COARSEN = 8
EXCHANGE = 0.05
TRACER_DIFF = 0.5

ZL, XC, CORE = 4, 4, 2
GROUP = XC * CORE
ROWS = 16
NY = 8192
CHUNKS = 8
WIDE = NY // CHUNKS
TILES = WIDE // 128
HALO = 8
BATCH = 4
FIRST = 1
FRAME = 28
F32 = jnp.float32
VMEM_LIMIT = 48 * 1024 * 1024


def lanes():
    return lax.broadcasted_iota(jnp.int32, (8, 128), 1)


def right_of(tiles, lane):
    first = pltpu.roll(tiles[0], 127, 1)
    return tiles[1:] + [jnp.where(lane == 127, pltpu.roll(first, 7, 0), first)]


def left_of(tiles, lane):
    last = pltpu.roll(tiles[-1], 1, 1)
    return [jnp.where(lane == 0, pltpu.roll(last, 1, 0), last)] + tiles[:-1]


def tile_at(r, t):
    return pl.ds(pl.multiple_of(r * 64 + t * 8, 8), 8)


def row_of(ref, r):
    return [ref[tile_at(r, t), :] for t in range(TILES)]


def permutation(inverse):
    a = lax.broadcasted_iota(jnp.int32, (WIDE, WIDE), 1 if inverse else 0)
    b = lax.broadcasted_iota(jnp.int32, (WIDE, WIDE), 0 if inverse else 1)
    return jnp.where((a % 8) * 128 + a // 8 == b, 1.0, 0.0).astype(jnp.bfloat16)


def permuted(x, order):
    total = None
    for _ in range(3):
        part = x.astype(jnp.bfloat16)
        x = x - part.astype(F32)
        moved = jnp.dot(part, order, preferred_element_type=F32)
        total = moved if total is None else total + moved
    return total


def to_frame(piece, out, order):
    x = jnp.concatenate([piece(slice(c * WIDE, (c + 1) * WIDE)) for c in range(CHUNKS)], axis=0)
    x = permuted(x, order)
    for c in range(CHUNKS):
        for t in range(TILES):
            out[pl.ds(t * 8 + c, 8, stride=64), :] = x[8 * c:8 * c + 8, 128 * t:128 * (t + 1)]


def sum_rows(ref, first):
    total = row_of(ref, first)
    for r in range(1, 8):
        total = [a + b for a, b in zip(total, row_of(ref, first + r))]
    return total


def restrict_sum(total):
    while len(total) > 1:
        total = [a + b for a, b in zip(total[::2], total[1::2])]
    return total[0] * (1.0 / (COARSEN * COARSEN))


def faces(k_ref, kr_ref, kd_ref):
    lane = lanes()

    def batch(i, _):
        k = row_of(k_ref, i * BATCH)
        for n in range(BATCH):
            r = i * BATCH + n
            below = row_of(k_ref, jnp.minimum(r + 1, FRAME - 1))
            right = right_of(k, lane)
            for t in range(TILES):
                kr_ref[tile_at(r, t), :] = 0.5 * (k[t] + right[t])
                kd_ref[tile_at(r, t), :] = 0.5 * (k[t] + below[t])
            k = below
        return 0

    lax.fori_loop(0, FRAME // BATCH, batch, 0)


def sweep(old, new, kr_ref, kd_ref, low, count):
    lane = lanes()

    def batch(i, _):
        base = low + i * BATCH
        flux = [None, None]
        for f in range(2):
            above = jnp.maximum(base - 1, 0)
            v, below, face = row_of(old[f], above), row_of(old[f], base), row_of(kd_ref, above)
            flux[f] = [face[t] * (below[t] - v[t]) for t in range(TILES)]
        for n in range(BATCH):
            r = base + n
            kr, kd = row_of(kr_ref, r), row_of(kd_ref, r)
            now, spread = [], []
            for f, ref in enumerate(old):
                v, below = row_of(ref, r), row_of(ref, r + 1)
                right = right_of(v, lane)
                side = [kr[t] * (right[t] - v[t]) for t in range(TILES)]
                left = left_of(side, lane)
                down = [kd[t] * (below[t] - v[t]) for t in range(TILES)]
                spread.append([(side[t] - left[t]) + (down[t] - flux[f][t]) for t in range(TILES)])
                flux[f] = down
                now.append(v)
            for t in range(TILES):
                move = EXCHANGE * (now[1][t] - now[0][t])
                new[0][tile_at(r, t), :] = now[0][t] + (spread[0][t] + move)
                new[1][tile_at(r, t), :] = now[1][t] + (TRACER_DIFF * spread[1][t] - move)
        return 0

    lax.fori_loop(0, (count + BATCH - 1) // BATCH, batch, 0)


def clear_outside(row, fields):
    @pl.when(row == 0)
    def _():
        for ref in fields:
            ref[pl.ds((FIRST + 7) * 64, 64), :] = jnp.zeros((64, 128), F32)

    @pl.when(row == ROWS - 1)
    def _():
        for ref in fields:
            ref[pl.ds((FIRST + 16) * 64, 64), :] = jnp.zeros((64, 128), F32)


def clear_margins(fields):
    for ref in fields:
        ref[0:FIRST * 64, :] = jnp.zeros((FIRST * 64, 128), F32)
        ref[(FIRST + 24) * 64:FRAME * 64, :] = jnp.zeros(((FRAME - FIRST - 24) * 64, 128), F32)


def conductivity_kernel(core_ref, k_ref, kf_ref, half_ref, kc_ref):
    to_frame(lambda c: k_ref[:, c], kf_ref, permutation(False))
    half_ref[...] = kf_ref[pl.ds(pl.multiple_of(core_ref[0] * 256, 256), 256), :]
    kc_ref[...] = restrict_sum(sum_rows(kf_ref, 0))


def start_kernel(u_ref, uf_ref, rs_ref):
    order = permutation(False)
    for f in range(2):
        to_frame(lambda c, f=f: u_ref[f, :, c], uf_ref.at[f], order)
        rs_ref[f] = restrict_sum(sum_rows(uf_ref.at[f], 0))


def conductivity_frame(core, k_ref, mine_ref, other_ref, k, kr, kd):
    clear_margins((k,))
    k[(FIRST + HALO) * 64:(FIRST + 2 * HALO) * 64, :] = k_ref[...]
    for part, half in ((mine_ref, core), (other_ref, 1 - core)):
        for side in range(2):
            at = (FIRST + 2 * HALO * side) * 64 + half * 256
            k[pl.ds(pl.multiple_of(at, 64), 256), :] = part[side]
    faces(k, kr, kd)


def steps(one, other, row, kr, kd, low, count, grow):
    def pair(i, _):
        for n, (old, new) in enumerate(((one, other), (other, one))):
            done = 2 * i + n
            sweep(old, new, kr, kd, FIRST + low - grow * done, count + 2 * grow * done)
            clear_outside(row, new)
        return 0

    lax.fori_loop(0, FINE // 2, pair, 0)


def local_kernel(place_ref, own_ref, k_ref, mine_ref, other_ref, rs_ref, kc_ref, out_ref, h, t, h2, t2, k, kr, kd, mix):
    lane = lanes()
    conductivity_frame(place_ref[1], k_ref, mine_ref, other_ref, k, kr, kd)
    for ref in (h, t, h2, t2):
        ref[...] = jnp.zeros_like(ref)
    for f, ref in enumerate((h, t)):
        ref[(FIRST + HALO) * 64:(FIRST + 2 * HALO) * 64, :] = own_ref[f]
    steps((h, t), (h2, t2), place_ref[0], kr, kd, HALO - 1, HALO + 2, 1)
    for b in range(3):
        for f, ref in enumerate((h, t)):
            mix[pl.ds(2 * b + f, 8, stride=8), :] = restrict_sum(sum_rows(ref, FIRST + HALO * b))
    for f in range(2):
        mix[pl.ds(6 + f, 8, stride=8), :] = rs_ref[f]
    kc = kc_ref[...]
    turned = pltpu.roll(kc, 64, 1)
    for j in range(ROWS):
        c, odd = j // 2, j % 2
        d = (c + 1) % CHUNKS if odd else (c - 1) % CHUNKS
        far = mix[8 * d:8 * d + 8, :]
        extra = jnp.concatenate([turned[c:c + 1], kc[c:c + 1], (turned if odd else kc)[d:d + 1], jnp.zeros((5, 128), F32)], axis=0)
        out_ref[j, 0:8, :] = mix[8 * c:8 * c + 8, :]
        out_ref[j, 8:16, :] = jnp.where(lane < 64, far if odd else pltpu.roll(far, 64, 1), extra)


def window_kernel(place_ref, got_ref, w_ref, rf_ref, kc_ref):
    odd = place_ref[2] % 2 == 1
    first = lax.broadcasted_iota(jnp.int32, (16, 128), 0)
    lane = lax.broadcasted_iota(jnp.int32, (16, 128), 1)

    def part(k):
        return got_ref[pl.ds(k, 16, stride=16), :]

    def tiles(full, low, high):
        half = jnp.where(odd, jnp.where(lane < 64, low, 0.0), jnp.where(lane < 64, 0.0, high))
        return jnp.where(odd, full, half), jnp.where(odd, half, full)

    def window(k):
        low = part(8 + k)
        return tiles(part(k), low, pltpu.roll(low, 64, 1))

    high = part(10)
    for s, x in enumerate(tiles(jnp.where(lane < 64, pltpu.roll(part(8), 64, 1), part(9)), pltpu.roll(high, 64, 1), high)):
        kc_ref[16 * s:16 * (s + 1), :] = x
    for f in range(2):
        up, own, down, later = window(f), window(2 + f), window(4 + f), window(6 + f)
        for s in range(2):
            total = own[s] + jnp.where(first == 0, 0.0, pltpu.roll(down[s], 1, 0))
            total = total + jnp.where(first == 15, 0.0, pltpu.roll(up[s], 15, 0))
            at = slice(32 * s + 16 * f, 32 * s + 16 * f + 16)
            rf_ref[at, :] = total
            w = total - later[s]
            for m in range(GROUP):
                w_ref[m, at, :] = w


def field(ref, f):
    return jnp.concatenate([ref[16 * f:16 * f + 16, :], ref[32 + 16 * f:48 + 16 * f, :]], axis=1)


def put(ref, f, x):
    ref[16 * f:16 * f + 16, :] = x[:, :128]
    ref[32 + 16 * f:48 + 16 * f, :] = x[:, 128:]


def coarse_coefficients(kc_ref):
    k = jnp.concatenate([kc_ref[0:16, :], kc_ref[16:32, :]], axis=1)
    width = k.shape[1]
    row = lax.broadcasted_iota(jnp.int32, k.shape, 0)
    scale = 0.5 * (FINE / COARSE) / (COARSEN * COARSEN)
    up = scale * (k + jnp.where(row == 0, 0.0, pltpu.roll(k, 1, 0)))
    down = scale * (k + jnp.where(row == 15, 0.0, pltpu.roll(k, 15, 0)))
    right = scale * (k + pltpu.roll(k, width - 1, 1))
    left = scale * (k + pltpu.roll(k, 1, 1))
    total = up + down + right + left
    keep = 1.0 - EXCHANGE * FINE / COARSE
    return (jnp.where(row == 0, 0.0, up), jnp.where(row == 15, 0.0, down), right, left,
            keep - total, keep - TRACER_DIFF * total)


def coarse_apply(e, coefficients):
    up, down, right, left, mid_h, mid_t = coefficients
    width = up.shape[1]
    trade = EXCHANGE * FINE / COARSE

    def around(v):
        return (up * pltpu.roll(v, 1, 0) + down * pltpu.roll(v, 15, 0)) + (
            right * pltpu.roll(v, width - 1, 1) + left * pltpu.roll(v, 1, 1))

    h, t = e
    for _ in range(COARSE):
        h, t = (around(h) + (mid_h * h + trade * t),
                TRACER_DIFF * around(t) + (mid_t * t + trade * h))
    return h, t


def group_kernel(place_ref, got_ref, kc_ref, sum_ref, own_ref):
    place = place_ref[0]
    coefficients = coarse_coefficients(kc_ref)
    shape = coefficients[0].shape
    zero = jnp.zeros(shape, F32)
    put(own_ref, 0, zero)
    put(own_ref, 1, zero)

    def link(m, e):
        @pl.when(m == place)
        def _():
            put(own_ref, 0, e[0])
            put(own_ref, 1, e[1])
        nxt = coarse_apply(e, coefficients)
        w = got_ref.at[m]
        return nxt[0] + field(w, 0), nxt[1] + field(w, 1)

    e = lax.fori_loop(0, GROUP, link, (zero, zero))
    for g in range(ZL):
        put(sum_ref.at[g], 0, e[0])
        put(sum_ref.at[g], 1, e[1])


def close_kernel(place_ref, got_ref, kc_ref, own_ref, rf_ref, out_ref):
    place, group, block = place_ref[0], place_ref[1], place_ref[2]
    coefficients = coarse_coefficients(kc_ref)
    zero = jnp.zeros(coefficients[0].shape, F32)

    def repeat(count, e):
        return lax.fori_loop(0, count, lambda _, x: coarse_apply(x, coefficients), e)

    def link(g, e):
        e = repeat(jnp.where(g == 0, 0, GROUP), e)
        got = got_ref.at[g]
        return e[0] + field(got, 0), e[1] + field(got, 1)

    e = lax.fori_loop(0, group, link, (zero, zero))
    e = repeat(jnp.where(group == 0, 0, place), e)
    e = coarse_apply((e[0] + field(own_ref, 0), e[1] + field(own_ref, 1)), coefficients)
    h, t = e[0] + field(rf_ref, 0), e[1] + field(rf_ref, 1)
    odd = block % 2 == 1
    lane = lax.broadcasted_iota(jnp.int32, (16, 128), 1)
    middle = [jnp.where(odd, pltpu.roll(x[:, :128], 64, 1), x[:, 128:]) for x in (h, t)]
    both = jnp.where(lane < 64, middle[0], pltpu.roll(middle[1], 64, 1))
    for j in range(ROWS):
        out_ref[j] = both


def fine_kernel(place_ref, own_ref, above_ref, below_ref, k_ref, mine_ref, other_ref, ends_ref, mean_ref, h, t, h2, t2, k, kr, kd):
    conductivity_frame(place_ref[1], k_ref, mine_ref, other_ref, k, kr, kd)
    clear_margins((h, t, h2, t2))
    for f, ref in enumerate((h, t)):
        for n, part in enumerate((above_ref, own_ref, below_ref)):
            at = (FIRST + n * HALO) * 64
            ref[at:at + HALO * 64, :] = part[f]
    steps((h, t), (h2, t2), place_ref[0], kr, kd, 1, 3 * HALO - 2, -1)
    back = permutation(True)
    for f, ref in enumerate((h, t)):
        mean_ref[f] = restrict_sum(sum_rows(ref, FIRST + HALO))
        x = jnp.concatenate([
            jnp.concatenate([ref[pl.ds((FIRST + HALO) * 64 + s * 8 + c, 8, stride=64), :] for s in range(TILES)], axis=1)
            for c in range(CHUNKS)], axis=0)
        x = permuted(x, back)
        for c in range(CHUNKS):
            ends_ref[f, :, c * WIDE:(c + 1) * WIDE] = x[8 * c:8 * c + 8, :]


def finish_kernel(place_ref, fine_ref, mean_ref, got_ref, ends_ref, next_ref):
    lane = lanes()
    row = place_ref[0]
    wide = lax.broadcasted_iota(jnp.int32, (16, 128), 1)
    for q in range(CHUNKS):
        even, odd = got_ref[32 * q:32 * q + 16, :], got_ref[32 * q + 16:32 * q + 32, :]
        cols = slice(128 * q, 128 * (q + 1))
        next_ref[0, :, cols] = jnp.where(wide < 64, even, pltpu.roll(odd, 64, 1))
        next_ref[1, :, cols] = jnp.where(wide < 64, pltpu.roll(even, 64, 1), odd)
    even = got_ref[pl.ds(row, 8, stride=32), :]
    odd = got_ref[pl.ds(row + 16, 8, stride=32), :]
    mine = (jnp.where(lane < 64, even, pltpu.roll(odd, 64, 1)), jnp.where(lane < 64, pltpu.roll(even, 64, 1), odd))
    for f in range(2):
        change = mine[f] - mean_ref[f]
        for t in range(TILES):
            spread = jnp.take_along_axis(change, 16 * t + lane // 8, axis=1)
            for c in range(CHUNKS):
                cols = slice(c * WIDE + 128 * t, c * WIDE + 128 * (t + 1))
                ends_ref[f, :, cols] = fine_ref[f, :, cols] + jnp.broadcast_to(spread[c:c + 1], (8, 128))


def call(kernel, outs, scratch, args, scalars=0, name=None, us=1):
    vmem = pl.BlockSpec(memory_space=pltpu.VMEM)
    specs = [pl.BlockSpec(memory_space=pltpu.SMEM)] * scalars + [vmem] * (len(args) - scalars)
    shapes = [jax.ShapeDtypeStruct(s, F32) for s in outs]
    single = len(outs) == 1
    return pl.pallas_call(
        kernel,
        out_shape=shapes[0] if single else shapes,
        in_specs=specs,
        out_specs=vmem if single else [vmem] * len(outs),
        scratch_shapes=[pltpu.VMEM(s, F32) for s in scratch],
        compiler_params=pltpu.CompilerParams(vmem_limit_bytes=VMEM_LIMIT),
        name=name,
        cost_estimate=pl.CostEstimate(flops=0, bytes_accessed=us * 3690000, transcendentals=0),
    )(*args)


def body(starts, conductivity):
    rows_axes, tm_axes = ("y", "z_hi"), ("z_lo", "x", "core")
    u = starts[0]
    row = lax.axis_index(rows_axes).astype(jnp.int32)
    group = lax.axis_index("z_lo").astype(jnp.int32)
    place = lax.axis_index(("x", "core")).astype(jnp.int32)
    core = lax.axis_index("core").astype(jnp.int32)
    here = jnp.stack([row, core])
    places = jnp.stack([place, group, row])

    def from_above(x):
        return lax.ppermute(x, rows_axes, [(i, i + 1) for i in range(ROWS - 1)])

    def from_below(x):
        return lax.ppermute(x, rows_axes, [(i + 1, i) for i in range(ROWS - 1)])

    kf, half, kc = call(conductivity_kernel, [(512, 128), (256, 128), (8, 128)], [], (core[None], conductivity), 1,
                        name="frame_conductivity", us=2)
    k_up, k_down = from_above(half), from_below(half)
    uf, rs = call(start_kernel, [(2, 512, 128), (2, 8, 128)], [], (u,), name="frame_starts", us=3)
    above, below = from_above(uf), from_below(uf)
    slices = ZL * GROUP
    rs_next = lax.ppermute(rs, tm_axes, [(i + 1, i) for i in range(slices - 1)])
    rs_next, k_up, k_down = lax.optimization_barrier((rs_next, k_up, k_down))
    mine = jnp.stack([k_up, k_down])
    other = lax.ppermute(mine, "core", [(0, 1), (1, 0)])
    frame = (FRAME * 64, 128)

    parts = call(local_kernel, [(ROWS, 16, 128)], [frame] * 7 + [(64, 128)],
                 (here, uf, kf, mine, other, rs_next, kc), 1, name="own_contributions", us=7)
    parts = lax.all_to_all(parts, rows_axes, 0, 0)
    parts = parts.reshape(ROWS * 16, 128)
    zero = row // 1024

    def chain(state):
        turn = state[0]
        where = places + turn * zero
        w, rf, kcw = call(window_kernel, [(GROUP, 64, 128), (64, 128), (32, 128)], [], (where, parts), 1, name="windows")
        w = lax.all_to_all(w, ("x", "core"), 0, 0)
        sums, own = call(group_kernel, [(ZL, 64, 128), (64, 128)], [], (where, w, kcw), 1, name="chain_in_group", us=3)
        sums = lax.all_to_all(sums, "z_lo", 0, 0)
        return turn + 1, call(close_kernel, [(ROWS, 16, 128)], [], (where, sums, kcw, own, rf), 1, name="chain_over_groups", us=4)

    _, after = lax.while_loop(lambda state: state[0] < 1 + zero, chain, (jnp.int32(0), jnp.zeros((ROWS, 16, 128), F32)))
    after = lax.all_to_all(after, rows_axes, 0, 0)
    fine, mean = call(fine_kernel, [(2, HALO, NY), (2, 8, 128)], [frame] * 7,
                      (here, uf, above, below, kf, mine, other), 1, name="fine_steps", us=9)
    ends, following = call(finish_kernel, [(2, HALO, NY), (2, ROWS, NY // COARSEN)], [],
                           (here, fine, mean, after.reshape(ROWS * 16, 128)), 1, name="ends", us=2)
    return ends[None], following[None]


def solution(mesh):
    fine_mesh = Mesh(mesh.devices.reshape(ZL, XC, CORE, 4, 4), ("z_lo", "x", "core", "y", "z_hi"))
    tm, rows = ("z_lo", "x", "core"), ("y", "z_hi")
    in_specs = (P(tm, None, rows, None), P(rows, None))
    out_specs = (P(tm, None, rows, None), P(tm, None, None, None))
    return jax.shard_map(body, mesh=fine_mesh, in_specs=in_specs, out_specs=out_specs, check_vma=False)
```

```python
import jax
import jax.numpy as jnp
from jax import lax
from jax.experimental import pallas as pl
from jax.experimental.pallas import tpu as pltpu
from jax.sharding import Mesh, PartitionSpec as P

FINE = 8
COARSE = 2
COARSEN = 8
EXCHANGE = 0.05
TRACER_DIFF = 0.5

ZL, XC, CORE = 4, 4, 2
GROUP = XC * CORE
ROWS = 16
NY = 8192
CHUNKS = 8
WIDE = NY // CHUNKS
TILES = WIDE // 128
HALO = 8
BATCH = 6
FIRST = 1
FRAME = 30
F32 = jnp.float32
VMEM_LIMIT = 48 * 1024 * 1024


def lanes():
    return lax.broadcasted_iota(jnp.int32, (8, 128), 1)


def right_of(tiles, lane):
    first = pltpu.roll(tiles[0], 127, 1)
    return tiles[1:] + [jnp.where(lane == 127, pltpu.roll(first, 7, 0), first)]


def left_of(tiles, lane):
    last = pltpu.roll(tiles[-1], 1, 1)
    return [jnp.where(lane == 0, pltpu.roll(last, 1, 0), last)] + tiles[:-1]


def tile_at(r, t):
    return pl.ds(pl.multiple_of(r * 64 + t * 8, 8), 8)


def row_of(ref, r):
    return [ref[tile_at(r, t), :] for t in range(TILES)]


def permutation(inverse):
    a = lax.broadcasted_iota(jnp.int32, (WIDE, WIDE), 1 if inverse else 0)
    b = lax.broadcasted_iota(jnp.int32, (WIDE, WIDE), 0 if inverse else 1)
    return jnp.where((a % 8) * 128 + a // 8 == b, 1.0, 0.0).astype(jnp.bfloat16)


def permuted(x, order):
    total = None
    for _ in range(3):
        part = x.astype(jnp.bfloat16)
        x = x - part.astype(F32)
        moved = jnp.dot(part, order, preferred_element_type=F32)
        total = moved if total is None else total + moved
    return total


def to_frame(piece, out, order):
    x = jnp.concatenate([piece(slice(c * WIDE, (c + 1) * WIDE)) for c in range(CHUNKS)], axis=0)
    x = permuted(x, order)
    for c in range(CHUNKS):
        for t in range(TILES):
            out[pl.ds(t * 8 + c, 8, stride=64), :] = x[8 * c:8 * c + 8, 128 * t:128 * (t + 1)]


def sum_rows(ref, first):
    total = row_of(ref, first)
    for r in range(1, 8):
        total = [a + b for a, b in zip(total, row_of(ref, first + r))]
    return total


def restrict_sum(total):
    while len(total) > 1:
        total = [a + b for a, b in zip(total[::2], total[1::2])]
    return total[0] * (1.0 / (COARSEN * COARSEN))


def faces(k_ref, kr_ref, kd_ref):
    lane = lanes()

    def batch(i, _):
        k = row_of(k_ref, i * BATCH)
        for n in range(BATCH):
            r = i * BATCH + n
            below = row_of(k_ref, jnp.minimum(r + 1, FRAME - 1))
            right = right_of(k, lane)
            for t in range(TILES):
                kr_ref[tile_at(r, t), :] = 0.5 * (k[t] + right[t])
                kd_ref[tile_at(r, t), :] = 0.5 * (k[t] + below[t])
            k = below
        return 0

    lax.fori_loop(0, FRAME // BATCH, batch, 0)


def sweep(old, new, kr_ref, kd_ref, low, count):
    lane = lanes()

    def batch(i, _):
        base = low + i * BATCH
        flux = [None, None]
        for f in range(2):
            above = jnp.maximum(base - 1, 0)
            v, below, face = row_of(old[f], above), row_of(old[f], base), row_of(kd_ref, above)
            flux[f] = [face[t] * (below[t] - v[t]) for t in range(TILES)]
        for n in range(BATCH):
            r = base + n
            kr, kd = row_of(kr_ref, r), row_of(kd_ref, r)
            now, spread = [], []
            for f, ref in enumerate(old):
                v, below = row_of(ref, r), row_of(ref, r + 1)
                right = right_of(v, lane)
                side = [kr[t] * (right[t] - v[t]) for t in range(TILES)]
                left = left_of(side, lane)
                down = [kd[t] * (below[t] - v[t]) for t in range(TILES)]
                spread.append([(side[t] - left[t]) + (down[t] - flux[f][t]) for t in range(TILES)])
                flux[f] = down
                now.append(v)
            for t in range(TILES):
                move = EXCHANGE * (now[1][t] - now[0][t])
                new[0][tile_at(r, t), :] = now[0][t] + (spread[0][t] + move)
                new[1][tile_at(r, t), :] = now[1][t] + (TRACER_DIFF * spread[1][t] - move)
        return 0

    lax.fori_loop(0, (count + BATCH - 1) // BATCH, batch, 0)


def clear_outside(row, fields):
    @pl.when(row == 0)
    def _():
        for ref in fields:
            ref[pl.ds((FIRST + 7) * 64, 64), :] = jnp.zeros((64, 128), F32)

    @pl.when(row == ROWS - 1)
    def _():
        for ref in fields:
            ref[pl.ds((FIRST + 16) * 64, 64), :] = jnp.zeros((64, 128), F32)


def clear_margins(fields):
    for ref in fields:
        ref[0:FIRST * 64, :] = jnp.zeros((FIRST * 64, 128), F32)
        ref[(FIRST + 24) * 64:FRAME * 64, :] = jnp.zeros(((FRAME - FIRST - 24) * 64, 128), F32)


def conductivity_kernel(core_ref, k_ref, kf_ref, half_ref, kc_ref):
    to_frame(lambda c: k_ref[:, c], kf_ref, permutation(False))
    half_ref[...] = kf_ref[pl.ds(pl.multiple_of(core_ref[0] * 256, 256), 256), :]
    kc_ref[...] = restrict_sum(sum_rows(kf_ref, 0))


def start_kernel(u_ref, uf_ref, rs_ref):
    order = permutation(False)
    for f in range(2):
        to_frame(lambda c, f=f: u_ref[f, :, c], uf_ref.at[f], order)
        rs_ref[f] = restrict_sum(sum_rows(uf_ref.at[f], 0))


def conductivity_frame(core, k_ref, mine_ref, other_ref, k, kr, kd):
    clear_margins((k,))
    k[(FIRST + HALO) * 64:(FIRST + 2 * HALO) * 64, :] = k_ref[...]
    for part, half in ((mine_ref, core), (other_ref, 1 - core)):
        for side in range(2):
            at = (FIRST + 2 * HALO * side) * 64 + half * 256
            k[pl.ds(pl.multiple_of(at, 64), 256), :] = part[side]
    faces(k, kr, kd)


def steps(one, other, row, kr, kd, low, count, grow):
    def pair(i, _):
        for n, (old, new) in enumerate(((one, other), (other, one))):
            done = 2 * i + n
            sweep(old, new, kr, kd, FIRST + low - grow * done, count + 2 * grow * done)
            clear_outside(row, new)
        return 0

    lax.fori_loop(0, FINE // 2, pair, 0)


def local_kernel(place_ref, own_ref, k_ref, mine_ref, other_ref, rs_ref, kc_ref, out_ref, h, t, h2, t2, k, kr, kd, mix):
    lane = lanes()
    conductivity_frame(place_ref[1], k_ref, mine_ref, other_ref, k, kr, kd)
    for ref in (h, t, h2, t2):
        ref[...] = jnp.zeros_like(ref)
    for f, ref in enumerate((h, t)):
        ref[(FIRST + HALO) * 64:(FIRST + 2 * HALO) * 64, :] = own_ref[f]
    steps((h, t), (h2, t2), place_ref[0], kr, kd, HALO - 1, HALO + 2, 1)
    for b in range(3):
        for f, ref in enumerate((h, t)):
            mix[pl.ds(2 * b + f, 8, stride=8), :] = restrict_sum(sum_rows(ref, FIRST + HALO * b))
    for f in range(2):
        mix[pl.ds(6 + f, 8, stride=8), :] = rs_ref[f]
    kc = kc_ref[...]
    turned = pltpu.roll(kc, 64, 1)
    for j in range(ROWS):
        c, odd = j // 2, j % 2
        d = (c + 1) % CHUNKS if odd else (c - 1) % CHUNKS
        far = mix[8 * d:8 * d + 8, :]
        extra = jnp.concatenate([turned[c:c + 1], kc[c:c + 1], (turned if odd else kc)[d:d + 1], jnp.zeros((5, 128), F32)], axis=0)
        out_ref[j, 0:8, :] = mix[8 * c:8 * c + 8, :]
        out_ref[j, 8:16, :] = jnp.where(lane < 64, far if odd else pltpu.roll(far, 64, 1), extra)


def window_kernel(place_ref, got_ref, w_ref, rf_ref, kc_ref):
    odd = place_ref[2] % 2 == 1
    first = lax.broadcasted_iota(jnp.int32, (16, 128), 0)
    lane = lax.broadcasted_iota(jnp.int32, (16, 128), 1)

    def part(k):
        return got_ref[pl.ds(k, 16, stride=16), :]

    def tiles(full, low, high):
        half = jnp.where(odd, jnp.where(lane < 64, low, 0.0), jnp.where(lane < 64, 0.0, high))
        return jnp.where(odd, full, half), jnp.where(odd, half, full)

    def window(k):
        low = part(8 + k)
        return tiles(part(k), low, pltpu.roll(low, 64, 1))

    high = part(10)
    for s, x in enumerate(tiles(jnp.where(lane < 64, pltpu.roll(part(8), 64, 1), part(9)), pltpu.roll(high, 64, 1), high)):
        kc_ref[16 * s:16 * (s + 1), :] = x
    for f in range(2):
        up, own, down, later = window(f), window(2 + f), window(4 + f), window(6 + f)
        for s in range(2):
            total = own[s] + jnp.where(first == 0, 0.0, pltpu.roll(down[s], 1, 0))
            total = total + jnp.where(first == 15, 0.0, pltpu.roll(up[s], 15, 0))
            at = slice(32 * s + 16 * f, 32 * s + 16 * f + 16)
            rf_ref[at, :] = total
            w = total - later[s]
            for m in range(GROUP):
                w_ref[m, at, :] = w


def field(ref, f):
    return jnp.concatenate([ref[16 * f:16 * f + 16, :], ref[32 + 16 * f:48 + 16 * f, :]], axis=1)


def put(ref, f, x):
    ref[16 * f:16 * f + 16, :] = x[:, :128]
    ref[32 + 16 * f:48 + 16 * f, :] = x[:, 128:]


def coarse_coefficients(kc_ref):
    k = jnp.concatenate([kc_ref[0:16, :], kc_ref[16:32, :]], axis=1)
    width = k.shape[1]
    row = lax.broadcasted_iota(jnp.int32, k.shape, 0)
    scale = 0.5 * (FINE / COARSE) / (COARSEN * COARSEN)
    up = scale * (k + jnp.where(row == 0, 0.0, pltpu.roll(k, 1, 0)))
    down = scale * (k + jnp.where(row == 15, 0.0, pltpu.roll(k, 15, 0)))
    right = scale * (k + pltpu.roll(k, width - 1, 1))
    left = scale * (k + pltpu.roll(k, 1, 1))
    total = up + down + right + left
    keep = 1.0 - EXCHANGE * FINE / COARSE
    return (jnp.where(row == 0, 0.0, up), jnp.where(row == 15, 0.0, down), right, left,
            keep - total, keep - TRACER_DIFF * total)


def coarse_apply(e, coefficients):
    up, down, right, left, mid_h, mid_t = coefficients
    width = up.shape[1]
    trade = EXCHANGE * FINE / COARSE

    def around(v):
        return (up * pltpu.roll(v, 1, 0) + down * pltpu.roll(v, 15, 0)) + (
            right * pltpu.roll(v, width - 1, 1) + left * pltpu.roll(v, 1, 1))

    h, t = e
    for _ in range(COARSE):
        h, t = (around(h) + (mid_h * h + trade * t),
                TRACER_DIFF * around(t) + (mid_t * t + trade * h))
    return h, t


def group_kernel(place_ref, got_ref, kc_ref, sum_ref, own_ref):
    place = place_ref[0]
    coefficients = coarse_coefficients(kc_ref)
    shape = coefficients[0].shape
    zero = jnp.zeros(shape, F32)
    put(own_ref, 0, zero)
    put(own_ref, 1, zero)

    def link(m, e):
        @pl.when(m == place)
        def _():
            put(own_ref, 0, e[0])
            put(own_ref, 1, e[1])
        nxt = coarse_apply(e, coefficients)
        w = got_ref.at[m]
        return nxt[0] + field(w, 0), nxt[1] + field(w, 1)

    e = lax.fori_loop(0, GROUP, link, (zero, zero))
    for g in range(ZL):
        put(sum_ref.at[g], 0, e[0])
        put(sum_ref.at[g], 1, e[1])


def close_kernel(place_ref, got_ref, kc_ref, own_ref, rf_ref, out_ref):
    place, group, block = place_ref[0], place_ref[1], place_ref[2]
    coefficients = coarse_coefficients(kc_ref)
    zero = jnp.zeros(coefficients[0].shape, F32)

    def repeat(count, e):
        return lax.fori_loop(0, count, lambda _, x: coarse_apply(x, coefficients), e)

    def link(g, e):
        e = repeat(jnp.where(g == 0, 0, GROUP), e)
        got = got_ref.at[g]
        return e[0] + field(got, 0), e[1] + field(got, 1)

    e = lax.fori_loop(0, group, link, (zero, zero))
    e = repeat(jnp.where(group == 0, 0, place), e)
    e = coarse_apply((e[0] + field(own_ref, 0), e[1] + field(own_ref, 1)), coefficients)
    h, t = e[0] + field(rf_ref, 0), e[1] + field(rf_ref, 1)
    odd = block % 2 == 1
    lane = lax.broadcasted_iota(jnp.int32, (16, 128), 1)
    middle = [jnp.where(odd, pltpu.roll(x[:, :128], 64, 1), x[:, 128:]) for x in (h, t)]
    both = jnp.where(lane < 64, middle[0], pltpu.roll(middle[1], 64, 1))
    for j in range(ROWS):
        out_ref[j] = both


def fine_kernel(place_ref, own_ref, above_ref, below_ref, k_ref, mine_ref, other_ref, ends_ref, mean_ref, h, t, h2, t2, k, kr, kd):
    conductivity_frame(place_ref[1], k_ref, mine_ref, other_ref, k, kr, kd)
    clear_margins((h, t, h2, t2))
    for f, ref in enumerate((h, t)):
        for n, part in enumerate((above_ref, own_ref, below_ref)):
            at = (FIRST + n * HALO) * 64
            ref[at:at + HALO * 64, :] = part[f]
    steps((h, t), (h2, t2), place_ref[0], kr, kd, 1, 3 * HALO - 2, -1)
    back = permutation(True)
    for f, ref in enumerate((h, t)):
        mean_ref[f] = restrict_sum(sum_rows(ref, FIRST + HALO))
        x = jnp.concatenate([
            jnp.concatenate([ref[pl.ds((FIRST + HALO) * 64 + s * 8 + c, 8, stride=64), :] for s in range(TILES)], axis=1)
            for c in range(CHUNKS)], axis=0)
        x = permuted(x, back)
        for c in range(CHUNKS):
            ends_ref[f, :, c * WIDE:(c + 1) * WIDE] = x[8 * c:8 * c + 8, :]


def finish_kernel(place_ref, fine_ref, mean_ref, got_ref, ends_ref, next_ref):
    lane = lanes()
    row = place_ref[0]
    wide = lax.broadcasted_iota(jnp.int32, (16, 128), 1)
    for q in range(CHUNKS):
        even, odd = got_ref[32 * q:32 * q + 16, :], got_ref[32 * q + 16:32 * q + 32, :]
        cols = slice(128 * q, 128 * (q + 1))
        next_ref[0, :, cols] = jnp.where(wide < 64, even, pltpu.roll(odd, 64, 1))
        next_ref[1, :, cols] = jnp.where(wide < 64, pltpu.roll(even, 64, 1), odd)
    even = got_ref[pl.ds(row, 8, stride=32), :]
    odd = got_ref[pl.ds(row + 16, 8, stride=32), :]
    mine = (jnp.where(lane < 64, even, pltpu.roll(odd, 64, 1)), jnp.where(lane < 64, pltpu.roll(even, 64, 1), odd))
    for f in range(2):
        change = mine[f] - mean_ref[f]
        for t in range(TILES):
            spread = jnp.take_along_axis(change, 16 * t + lane // 8, axis=1)
            for c in range(CHUNKS):
                cols = slice(c * WIDE + 128 * t, c * WIDE + 128 * (t + 1))
                ends_ref[f, :, cols] = fine_ref[f, :, cols] + jnp.broadcast_to(spread[c:c + 1], (8, 128))


def call(kernel, outs, scratch, args, scalars=0, name=None, us=1):
    vmem = pl.BlockSpec(memory_space=pltpu.VMEM)
    specs = [pl.BlockSpec(memory_space=pltpu.SMEM)] * scalars + [vmem] * (len(args) - scalars)
    shapes = [jax.ShapeDtypeStruct(s, F32) for s in outs]
    single = len(outs) == 1
    return pl.pallas_call(
        kernel,
        out_shape=shapes[0] if single else shapes,
        in_specs=specs,
        out_specs=vmem if single else [vmem] * len(outs),
        scratch_shapes=[pltpu.VMEM(s, F32) for s in scratch],
        compiler_params=pltpu.CompilerParams(vmem_limit_bytes=VMEM_LIMIT),
        name=name,
        cost_estimate=pl.CostEstimate(flops=0, bytes_accessed=us * 3690000, transcendentals=0),
    )(*args)


def body(starts, conductivity):
    rows_axes, tm_axes = ("y", "z_hi"), ("z_lo", "x", "core")
    u = starts[0]
    row = lax.axis_index(rows_axes).astype(jnp.int32)
    group = lax.axis_index("z_lo").astype(jnp.int32)
    place = lax.axis_index(("x", "core")).astype(jnp.int32)
    core = lax.axis_index("core").astype(jnp.int32)
    here = jnp.stack([row, core])
    places = jnp.stack([place, group, row])

    def from_above(x):
        return lax.ppermute(x, rows_axes, [(i, i + 1) for i in range(ROWS - 1)])

    def from_below(x):
        return lax.ppermute(x, rows_axes, [(i + 1, i) for i in range(ROWS - 1)])

    kf, half, kc = call(conductivity_kernel, [(512, 128), (256, 128), (8, 128)], [], (core[None], conductivity), 1,
                        name="frame_conductivity", us=2)
    k_up, k_down = from_above(half), from_below(half)
    uf, rs = call(start_kernel, [(2, 512, 128), (2, 8, 128)], [], (u,), name="frame_starts", us=3)
    above, below = from_above(uf), from_below(uf)
    slices = ZL * GROUP
    rs_next = lax.ppermute(rs, tm_axes, [(i + 1, i) for i in range(slices - 1)])
    rs_next, k_up, k_down = lax.optimization_barrier((rs_next, k_up, k_down))
    mine = jnp.stack([k_up, k_down])
    other = lax.ppermute(mine, "core", [(0, 1), (1, 0)])
    frame = (FRAME * 64, 128)

    parts = call(local_kernel, [(ROWS, 16, 128)], [frame] * 7 + [(64, 128)],
                 (here, uf, kf, mine, other, rs_next, kc), 1, name="own_contributions", us=7)
    parts = lax.all_to_all(parts, rows_axes, 0, 0)
    parts = parts.reshape(ROWS * 16, 128)
    zero = row // 1024

    def chain(state):
        turn = state[0]
        where = places + turn * zero
        w, rf, kcw = call(window_kernel, [(GROUP, 64, 128), (64, 128), (32, 128)], [], (where, parts), 1, name="windows")
        w = lax.all_to_all(w, ("x", "core"), 0, 0)
        sums, own = call(group_kernel, [(ZL, 64, 128), (64, 128)], [], (where, w, kcw), 1, name="chain_in_group", us=3)
        sums = lax.all_to_all(sums, "z_lo", 0, 0)
        return turn + 1, call(close_kernel, [(ROWS, 16, 128)], [], (where, sums, kcw, own, rf), 1, name="chain_over_groups", us=4)

    _, after = lax.while_loop(lambda state: state[0] < 1 + zero, chain, (jnp.int32(0), jnp.zeros((ROWS, 16, 128), F32)))
    after = lax.all_to_all(after, rows_axes, 0, 0)
    fine, mean = call(fine_kernel, [(2, HALO, NY), (2, 8, 128)], [frame] * 7,
                      (here, uf, above, below, kf, mine, other), 1, name="fine_steps", us=9)
    ends, following = call(finish_kernel, [(2, HALO, NY), (2, ROWS, NY // COARSEN)], [],
                           (here, fine, mean, after.reshape(ROWS * 16, 128)), 1, name="ends", us=2)
    return ends[None], following[None]


def solution(mesh):
    fine_mesh = Mesh(mesh.devices.reshape(ZL, XC, CORE, 4, 4), ("z_lo", "x", "core", "y", "z_hi"))
    tm, rows = ("z_lo", "x", "core"), ("y", "z_hi")
    in_specs = (P(tm, None, rows, None), P(rows, None))
    out_specs = (P(tm, None, rows, None), P(tm, None, None, None))
    return jax.shard_map(body, mesh=fine_mesh, in_specs=in_specs, out_specs=out_specs, check_vma=False)
```

```python
import jax
import jax.numpy as jnp
from jax import lax
from jax.experimental import pallas as pl
from jax.experimental.pallas import tpu as pltpu
from jax.sharding import Mesh, PartitionSpec as P

FINE = 8
COARSE = 2
COARSEN = 8
EXCHANGE = 0.05
TRACER_DIFF = 0.5

ZL, XC, CORE = 4, 4, 2
GROUP = XC * CORE
ROWS = 16
NY = 8192
CHUNKS = 8
WIDE = NY // CHUNKS
TILES = WIDE // 128
HALO = 8
BATCH = 6
FIRST = 1
FRAME = 30
F32 = jnp.float32
VMEM_LIMIT = 48 * 1024 * 1024


def lanes():
    return lax.broadcasted_iota(jnp.int32, (8, 128), 1)


def right_of(tiles, lane):
    first = pltpu.roll(tiles[0], 127, 1)
    return tiles[1:] + [jnp.where(lane == 127, pltpu.roll(first, 7, 0), first)]


def left_of(tiles, lane):
    last = pltpu.roll(tiles[-1], 1, 1)
    return [jnp.where(lane == 0, pltpu.roll(last, 1, 0), last)] + tiles[:-1]


def tile_at(r, t):
    return pl.ds(pl.multiple_of(r * 64 + t * 8, 8), 8)


def row_of(ref, r):
    return [ref[tile_at(r, t), :] for t in range(TILES)]


def permutation(inverse):
    a = lax.broadcasted_iota(jnp.int32, (WIDE, WIDE), 1 if inverse else 0)
    b = lax.broadcasted_iota(jnp.int32, (WIDE, WIDE), 0 if inverse else 1)
    return jnp.where((a % 8) * 128 + a // 8 == b, 1.0, 0.0).astype(jnp.bfloat16)


def permuted(x, order):
    total = None
    for _ in range(3):
        part = x.astype(jnp.bfloat16)
        x = x - part.astype(F32)
        moved = jnp.dot(part, order, preferred_element_type=F32)
        total = moved if total is None else total + moved
    return total


def to_frame(piece, out, order):
    x = jnp.concatenate([piece(slice(c * WIDE, (c + 1) * WIDE)) for c in range(CHUNKS)], axis=0)
    x = permuted(x, order)
    for c in range(CHUNKS):
        for t in range(TILES):
            out[pl.ds(t * 8 + c, 8, stride=64), :] = x[8 * c:8 * c + 8, 128 * t:128 * (t + 1)]


def sum_rows(ref, first):
    total = row_of(ref, first)
    for r in range(1, 8):
        total = [a + b for a, b in zip(total, row_of(ref, first + r))]
    return total


def restrict_sum(total):
    while len(total) > 1:
        total = [a + b for a, b in zip(total[::2], total[1::2])]
    return total[0] * (1.0 / (COARSEN * COARSEN))


def faces(k_ref, kr_ref, kd_ref):
    lane = lanes()

    def batch(i, _):
        k = row_of(k_ref, i * BATCH)
        for n in range(BATCH):
            r = i * BATCH + n
            below = row_of(k_ref, jnp.minimum(r + 1, FRAME - 1))
            right = right_of(k, lane)
            for t in range(TILES):
                kr_ref[tile_at(r, t), :] = 0.5 * (k[t] + right[t])
                kd_ref[tile_at(r, t), :] = 0.5 * (k[t] + below[t])
            k = below
        return 0

    lax.fori_loop(0, FRAME // BATCH, batch, 0)


def sweep(old, new, kr_ref, kd_ref, low, count):
    lane = lanes()

    def batch(i, _):
        base = low + i * BATCH
        flux = [None, None]
        for f in range(2):
            above = jnp.maximum(base - 1, 0)
            v, below, face = row_of(old[f], above), row_of(old[f], base), row_of(kd_ref, above)
            flux[f] = [face[t] * (below[t] - v[t]) for t in range(TILES)]
        for n in range(BATCH):
            r = base + n
            kr, kd = row_of(kr_ref, r), row_of(kd_ref, r)
            now, spread = [], []
            for f, ref in enumerate(old):
                v, below = row_of(ref, r), row_of(ref, r + 1)
                right = right_of(v, lane)
                side = [kr[t] * (right[t] - v[t]) for t in range(TILES)]
                left = left_of(side, lane)
                down = [kd[t] * (below[t] - v[t]) for t in range(TILES)]
                spread.append([(side[t] - left[t]) + (down[t] - flux[f][t]) for t in range(TILES)])
                flux[f] = down
                now.append(v)
            for t in range(TILES):
                move = EXCHANGE * (now[1][t] - now[0][t])
                new[0][tile_at(r, t), :] = now[0][t] + (spread[0][t] + move)
                new[1][tile_at(r, t), :] = now[1][t] + (TRACER_DIFF * spread[1][t] - move)
        return 0

    lax.fori_loop(0, (count + BATCH - 1) // BATCH, batch, 0)


def clear_outside(row, fields):
    @pl.when(row == 0)
    def _():
        for ref in fields:
            ref[pl.ds((FIRST + 7) * 64, 64), :] = jnp.zeros((64, 128), F32)

    @pl.when(row == ROWS - 1)
    def _():
        for ref in fields:
            ref[pl.ds((FIRST + 16) * 64, 64), :] = jnp.zeros((64, 128), F32)


def clear_margins(fields):
    for ref in fields:
        ref[0:FIRST * 64, :] = jnp.zeros((FIRST * 64, 128), F32)
        ref[(FIRST + 24) * 64:FRAME * 64, :] = jnp.zeros(((FRAME - FIRST - 24) * 64, 128), F32)


def conductivity_kernel(core_ref, k_ref, kf_ref, half_ref, kc_ref):
    to_frame(lambda c: k_ref[:, c], kf_ref, permutation(False))
    half_ref[...] = kf_ref[pl.ds(pl.multiple_of(core_ref[0] * 256, 256), 256), :]
    kc_ref[...] = restrict_sum(sum_rows(kf_ref, 0))


def start_kernel(u_ref, uf_ref, rs_ref):
    order = permutation(False)
    for f in range(2):
        to_frame(lambda c, f=f: u_ref[f, :, c], uf_ref.at[f], order)
        rs_ref[f] = restrict_sum(sum_rows(uf_ref.at[f], 0))


def conductivity_frame(core, k_ref, mine_ref, other_ref, k, kr, kd):
    clear_margins((k,))
    k[(FIRST + HALO) * 64:(FIRST + 2 * HALO) * 64, :] = k_ref[...]
    for part, half in ((mine_ref, core), (other_ref, 1 - core)):
        for side in range(2):
            at = (FIRST + 2 * HALO * side) * 64 + half * 256
            k[pl.ds(pl.multiple_of(at, 64), 256), :] = part[side]
    faces(k, kr, kd)


def steps(one, other, row, kr, kd, low, count, grow):
    def pair(i, _):
        for n, (old, new) in enumerate(((one, other), (other, one))):
            done = 2 * i + n
            sweep(old, new, kr, kd, FIRST + low - grow * done, count + 2 * grow * done)
            clear_outside(row, new)
        return 0

    lax.fori_loop(0, FINE // 2, pair, 0)


def local_kernel(place_ref, own_ref, k_ref, mine_ref, other_ref, rs_ref, kc_ref, out_ref, h, t, h2, t2, k, kr, kd, mix):
    lane = lanes()
    conductivity_frame(place_ref[1], k_ref, mine_ref, other_ref, k, kr, kd)
    for ref in (h, t, h2, t2):
        ref[...] = jnp.zeros_like(ref)
    for f, ref in enumerate((h, t)):
        ref[(FIRST + HALO) * 64:(FIRST + 2 * HALO) * 64, :] = own_ref[f]
    steps((h, t), (h2, t2), place_ref[0], kr, kd, HALO - 1, HALO + 2, 1)
    for b in range(3):
        for f, ref in enumerate((h, t)):
            mix[pl.ds(2 * b + f, 8, stride=8), :] = restrict_sum(sum_rows(ref, FIRST + HALO * b))
    for f in range(2):
        mix[pl.ds(6 + f, 8, stride=8), :] = rs_ref[f]
    kc = kc_ref[...]
    turned = pltpu.roll(kc, 64, 1)
    for j in range(ROWS):
        c, odd = j // 2, j % 2
        d = (c + 1) % CHUNKS if odd else (c - 1) % CHUNKS
        far = mix[8 * d:8 * d + 8, :]
        extra = jnp.concatenate([turned[c:c + 1], kc[c:c + 1], (turned if odd else kc)[d:d + 1], jnp.zeros((5, 128), F32)], axis=0)
        out_ref[j, 0:8, :] = mix[8 * c:8 * c + 8, :]
        out_ref[j, 8:16, :] = jnp.where(lane < 64, far if odd else pltpu.roll(far, 64, 1), extra)


def window_kernel(place_ref, got_ref, w_ref, rf_ref, kc_ref):
    odd = place_ref[2] % 2 == 1
    first = lax.broadcasted_iota(jnp.int32, (16, 128), 0)
    lane = lax.broadcasted_iota(jnp.int32, (16, 128), 1)

    def part(k):
        return got_ref[pl.ds(k, 16, stride=16), :]

    def tiles(full, low, high):
        half = jnp.where(odd, jnp.where(lane < 64, low, 0.0), jnp.where(lane < 64, 0.0, high))
        return jnp.where(odd, full, half), jnp.where(odd, half, full)

    def window(k):
        low = part(8 + k)
        return tiles(part(k), low, pltpu.roll(low, 64, 1))

    high = part(10)
    for s, x in enumerate(tiles(jnp.where(lane < 64, pltpu.roll(part(8), 64, 1), part(9)), pltpu.roll(high, 64, 1), high)):
        kc_ref[16 * s:16 * (s + 1), :] = x
    for f in range(2):
        up, own, down, later = window(f), window(2 + f), window(4 + f), window(6 + f)
        for s in range(2):
            total = own[s] + jnp.where(first == 0, 0.0, pltpu.roll(down[s], 1, 0))
            total = total + jnp.where(first == 15, 0.0, pltpu.roll(up[s], 15, 0))
            at = slice(32 * s + 16 * f, 32 * s + 16 * f + 16)
            rf_ref[at, :] = total
            w = total - later[s]
            for m in range(GROUP):
                w_ref[m, at, :] = w


def field(ref, f):
    return jnp.concatenate([ref[16 * f:16 * f + 16, :], ref[32 + 16 * f:48 + 16 * f, :]], axis=1)


def put(ref, f, x):
    ref[16 * f:16 * f + 16, :] = x[:, :128]
    ref[32 + 16 * f:48 + 16 * f, :] = x[:, 128:]


def coarse_coefficients(kc_ref):
    k = jnp.concatenate([kc_ref[0:16, :], kc_ref[16:32, :]], axis=1)
    width = k.shape[1]
    row = lax.broadcasted_iota(jnp.int32, k.shape, 0)
    scale = 0.5 * (FINE / COARSE) / (COARSEN * COARSEN)
    up = scale * (k + jnp.where(row == 0, 0.0, pltpu.roll(k, 1, 0)))
    down = scale * (k + jnp.where(row == 15, 0.0, pltpu.roll(k, 15, 0)))
    right = scale * (k + pltpu.roll(k, width - 1, 1))
    left = scale * (k + pltpu.roll(k, 1, 1))
    total = up + down + right + left
    keep = 1.0 - EXCHANGE * FINE / COARSE
    return (jnp.where(row == 0, 0.0, up), jnp.where(row == 15, 0.0, down), right, left,
            keep - total, keep - TRACER_DIFF * total)


def coarse_apply(e, coefficients):
    up, down, right, left, mid_h, mid_t = coefficients
    width = up.shape[1]
    trade = EXCHANGE * FINE / COARSE

    def around(v):
        return (up * pltpu.roll(v, 1, 0) + down * pltpu.roll(v, 15, 0)) + (
            right * pltpu.roll(v, width - 1, 1) + left * pltpu.roll(v, 1, 1))

    h, t = e
    for _ in range(COARSE):
        h, t = (around(h) + (mid_h * h + trade * t),
                TRACER_DIFF * around(t) + (mid_t * t + trade * h))
    return h, t


def group_kernel(place_ref, got_ref, kc_ref, sum_ref, own_ref):
    place, group = place_ref[0], place_ref[1]
    coefficients = coarse_coefficients(kc_ref)
    shape = coefficients[0].shape
    zero = jnp.zeros(shape, F32)
    put(own_ref, 0, zero)
    put(own_ref, 1, zero)

    def link(m, e):
        @pl.when(m == place)
        def _():
            put(own_ref, 0, e[0])
            put(own_ref, 1, e[1])
        nxt = coarse_apply(e, coefficients)
        w = got_ref.at[m]
        return nxt[0] + field(w, 0), nxt[1] + field(w, 1)

    e = lax.fori_loop(0, GROUP, link, (zero, zero))
    ahead = [e]
    for _ in range(ZL - 2):
        ahead.append(lax.fori_loop(0, GROUP, lambda _, x: coarse_apply(x, coefficients), ahead[-1]))
    for g in range(ZL):
        for f in range(2):
            x = zero
            for gap in range(1, ZL):
                x = jnp.where(g - group == gap, ahead[gap - 1][f], x)
            put(sum_ref.at[g], f, x)


def close_kernel(place_ref, got_ref, kc_ref, own_ref, rf_ref, out_ref):
    place, group, block = place_ref[0], place_ref[1], place_ref[2]
    coefficients = coarse_coefficients(kc_ref)
    e = tuple(sum(field(got_ref.at[g], f) for g in range(ZL)) for f in range(2))
    e = lax.fori_loop(0, jnp.where(group == 0, 0, place), lambda _, x: coarse_apply(x, coefficients), e)
    e = coarse_apply((e[0] + field(own_ref, 0), e[1] + field(own_ref, 1)), coefficients)
    h, t = e[0] + field(rf_ref, 0), e[1] + field(rf_ref, 1)
    odd = block % 2 == 1
    lane = lax.broadcasted_iota(jnp.int32, (16, 128), 1)
    middle = [jnp.where(odd, pltpu.roll(x[:, :128], 64, 1), x[:, 128:]) for x in (h, t)]
    both = jnp.where(lane < 64, middle[0], pltpu.roll(middle[1], 64, 1))
    for j in range(ROWS):
        out_ref[j] = both


def fine_kernel(place_ref, own_ref, above_ref, below_ref, k_ref, mine_ref, other_ref, ends_ref, mean_ref, h, t, h2, t2, k, kr, kd):
    conductivity_frame(place_ref[1], k_ref, mine_ref, other_ref, k, kr, kd)
    clear_margins((h, t, h2, t2))
    for f, ref in enumerate((h, t)):
        for n, part in enumerate((above_ref, own_ref, below_ref)):
            at = (FIRST + n * HALO) * 64
            ref[at:at + HALO * 64, :] = part[f]
    steps((h, t), (h2, t2), place_ref[0], kr, kd, 1, 3 * HALO - 2, -1)
    back = permutation(True)
    for f, ref in enumerate((h, t)):
        mean_ref[f] = restrict_sum(sum_rows(ref, FIRST + HALO))
        x = jnp.concatenate([
            jnp.concatenate([ref[pl.ds((FIRST + HALO) * 64 + s * 8 + c, 8, stride=64), :] for s in range(TILES)], axis=1)
            for c in range(CHUNKS)], axis=0)
        x = permuted(x, back)
        for c in range(CHUNKS):
            ends_ref[f, :, c * WIDE:(c + 1) * WIDE] = x[8 * c:8 * c + 8, :]


def finish_kernel(place_ref, fine_ref, mean_ref, got_ref, ends_ref, next_ref):
    lane = lanes()
    row = place_ref[0]
    wide = lax.broadcasted_iota(jnp.int32, (16, 128), 1)
    for q in range(CHUNKS):
        even, odd = got_ref[32 * q:32 * q + 16, :], got_ref[32 * q + 16:32 * q + 32, :]
        cols = slice(128 * q, 128 * (q + 1))
        next_ref[0, :, cols] = jnp.where(wide < 64, even, pltpu.roll(odd, 64, 1))
        next_ref[1, :, cols] = jnp.where(wide < 64, pltpu.roll(even, 64, 1), odd)
    even = got_ref[pl.ds(row, 8, stride=32), :]
    odd = got_ref[pl.ds(row + 16, 8, stride=32), :]
    mine = (jnp.where(lane < 64, even, pltpu.roll(odd, 64, 1)), jnp.where(lane < 64, pltpu.roll(even, 64, 1), odd))
    for f in range(2):
        change = mine[f] - mean_ref[f]
        for t in range(TILES):
            spread = jnp.take_along_axis(change, 16 * t + lane // 8, axis=1)
            for c in range(CHUNKS):
                cols = slice(c * WIDE + 128 * t, c * WIDE + 128 * (t + 1))
                ends_ref[f, :, cols] = fine_ref[f, :, cols] + jnp.broadcast_to(spread[c:c + 1], (8, 128))


def call(kernel, outs, scratch, args, scalars=0, name=None, us=1):
    vmem = pl.BlockSpec(memory_space=pltpu.VMEM)
    specs = [pl.BlockSpec(memory_space=pltpu.SMEM)] * scalars + [vmem] * (len(args) - scalars)
    shapes = [jax.ShapeDtypeStruct(s, F32) for s in outs]
    single = len(outs) == 1
    return pl.pallas_call(
        kernel,
        out_shape=shapes[0] if single else shapes,
        in_specs=specs,
        out_specs=vmem if single else [vmem] * len(outs),
        scratch_shapes=[pltpu.VMEM(s, F32) for s in scratch],
        compiler_params=pltpu.CompilerParams(vmem_limit_bytes=VMEM_LIMIT),
        name=name,
        cost_estimate=pl.CostEstimate(flops=0, bytes_accessed=us * 3690000, transcendentals=0),
    )(*args)


def body(starts, conductivity):
    rows_axes, tm_axes = ("y", "z_hi"), ("z_lo", "x", "core")
    u = starts[0]
    row = lax.axis_index(rows_axes).astype(jnp.int32)
    group = lax.axis_index("z_lo").astype(jnp.int32)
    place = lax.axis_index(("x", "core")).astype(jnp.int32)
    core = lax.axis_index("core").astype(jnp.int32)
    here = jnp.stack([row, core])
    places = jnp.stack([place, group, row])

    def from_above(x):
        return lax.ppermute(x, rows_axes, [(i, i + 1) for i in range(ROWS - 1)])

    def from_below(x):
        return lax.ppermute(x, rows_axes, [(i + 1, i) for i in range(ROWS - 1)])

    kf, half, kc = call(conductivity_kernel, [(512, 128), (256, 128), (8, 128)], [], (core[None], conductivity), 1,
                        name="frame_conductivity", us=2)
    k_up, k_down = from_above(half), from_below(half)
    uf, rs = call(start_kernel, [(2, 512, 128), (2, 8, 128)], [], (u,), name="frame_starts", us=3)
    above, below = from_above(uf), from_below(uf)
    slices = ZL * GROUP
    rs_next = lax.ppermute(rs, tm_axes, [(i + 1, i) for i in range(slices - 1)])
    rs_next, k_up, k_down = lax.optimization_barrier((rs_next, k_up, k_down))
    mine = jnp.stack([k_up, k_down])
    other = lax.ppermute(mine, "core", [(0, 1), (1, 0)])
    frame = (FRAME * 64, 128)

    parts = call(local_kernel, [(ROWS, 16, 128)], [frame] * 7 + [(64, 128)],
                 (here, uf, kf, mine, other, rs_next, kc), 1, name="own_contributions", us=7)
    parts = lax.all_to_all(parts, rows_axes, 0, 0)
    parts = parts.reshape(ROWS * 16, 128)
    zero = row // 1024

    def chain(state):
        turn = state[0]
        where = places + turn * zero
        w, rf, kcw = call(window_kernel, [(GROUP, 64, 128), (64, 128), (32, 128)], [], (where, parts), 1, name="windows")
        w = lax.all_to_all(w, ("x", "core"), 0, 0)
        sums, own = call(group_kernel, [(ZL, 64, 128), (64, 128)], [], (where, w, kcw), 1, name="chain_in_group", us=3)
        sums = lax.all_to_all(sums, "z_lo", 0, 0)
        return turn + 1, call(close_kernel, [(ROWS, 16, 128)], [], (where, sums, kcw, own, rf), 1, name="chain_over_groups", us=4)

    _, after = lax.while_loop(lambda state: state[0] < 1 + zero, chain, (jnp.int32(0), jnp.zeros((ROWS, 16, 128), F32)))
    after = lax.all_to_all(after, rows_axes, 0, 0)
    fine, mean = call(fine_kernel, [(2, HALO, NY), (2, 8, 128)], [frame] * 7,
                      (here, uf, above, below, kf, mine, other), 1, name="fine_steps", us=9)
    ends, following = call(finish_kernel, [(2, HALO, NY), (2, ROWS, NY // COARSEN)], [],
                           (here, fine, mean, after.reshape(ROWS * 16, 128)), 1, name="ends", us=2)
    return ends[None], following[None]


def solution(mesh):
    fine_mesh = Mesh(mesh.devices.reshape(ZL, XC, CORE, 4, 4), ("z_lo", "x", "core", "y", "z_hi"))
    tm, rows = ("z_lo", "x", "core"), ("y", "z_hi")
    in_specs = (P(tm, None, rows, None), P(rows, None))
    out_specs = (P(tm, None, rows, None), P(tm, None, None, None))
    return jax.shard_map(body, mesh=fine_mesh, in_specs=in_specs, out_specs=out_specs, check_vma=False)
```

```python
import jax
import jax.numpy as jnp
from jax import lax
from jax.experimental import pallas as pl
from jax.experimental.pallas import tpu as pltpu
from jax.sharding import Mesh, PartitionSpec as P

FINE = 8
COARSE = 2
COARSEN = 8
EXCHANGE = 0.05
TRACER_DIFF = 0.5

ZL, XC, CORE = 4, 4, 2
GROUP = XC * CORE
ROWS = 16
NY = 8192
CHUNKS = 8
WIDE = NY // CHUNKS
TILES = WIDE // 128
HALO = 8
BATCH = 8
FIRST = 1
FRAME = 32
F32 = jnp.float32
VMEM_LIMIT = 48 * 1024 * 1024


def lanes():
    return lax.broadcasted_iota(jnp.int32, (8, 128), 1)


def right_of(tiles, lane):
    first = pltpu.roll(tiles[0], 127, 1)
    return tiles[1:] + [jnp.where(lane == 127, pltpu.roll(first, 7, 0), first)]


def left_of(tiles, lane):
    last = pltpu.roll(tiles[-1], 1, 1)
    return [jnp.where(lane == 0, pltpu.roll(last, 1, 0), last)] + tiles[:-1]


def tile_at(r, t):
    return pl.ds(pl.multiple_of(r * 64 + t * 8, 8), 8)


def row_of(ref, r):
    return [ref[tile_at(r, t), :] for t in range(TILES)]


def permutation(inverse):
    a = lax.broadcasted_iota(jnp.int32, (WIDE, WIDE), 1 if inverse else 0)
    b = lax.broadcasted_iota(jnp.int32, (WIDE, WIDE), 0 if inverse else 1)
    return jnp.where((a % 8) * 128 + a // 8 == b, 1.0, 0.0).astype(jnp.bfloat16)


def permuted(x, order):
    total = None
    for _ in range(3):
        part = x.astype(jnp.bfloat16)
        x = x - part.astype(F32)
        moved = jnp.dot(part, order, preferred_element_type=F32)
        total = moved if total is None else total + moved
    return total


def to_frame(piece, out, order):
    x = jnp.concatenate([piece(slice(c * WIDE, (c + 1) * WIDE)) for c in range(CHUNKS)], axis=0)
    x = permuted(x, order)
    for c in range(CHUNKS):
        for t in range(TILES):
            out[pl.ds(t * 8 + c, 8, stride=64), :] = x[8 * c:8 * c + 8, 128 * t:128 * (t + 1)]


def sum_rows(ref, first):
    total = row_of(ref, first)
    for r in range(1, 8):
        total = [a + b for a, b in zip(total, row_of(ref, first + r))]
    return total


def restrict_sum(total):
    while len(total) > 1:
        total = [a + b for a, b in zip(total[::2], total[1::2])]
    return total[0] * (1.0 / (COARSEN * COARSEN))


def faces(k_ref, kr_ref, kd_ref):
    lane = lanes()

    def batch(i, _):
        k = row_of(k_ref, i * BATCH)
        for n in range(BATCH):
            r = i * BATCH + n
            below = row_of(k_ref, jnp.minimum(r + 1, FRAME - 1))
            right = right_of(k, lane)
            for t in range(TILES):
                kr_ref[tile_at(r, t), :] = 0.5 * (k[t] + right[t])
                kd_ref[tile_at(r, t), :] = 0.5 * (k[t] + below[t])
            k = below
        return 0

    lax.fori_loop(0, FRAME // BATCH, batch, 0)


def sweep(old, new, kr_ref, kd_ref, low, count):
    lane = lanes()

    def batch(i, _):
        base = low + i * BATCH
        flux = [None, None]
        for f in range(2):
            above = jnp.maximum(base - 1, 0)
            v, below, face = row_of(old[f], above), row_of(old[f], base), row_of(kd_ref, above)
            flux[f] = [face[t] * (below[t] - v[t]) for t in range(TILES)]
        for n in range(BATCH):
            r = base + n
            kr, kd = row_of(kr_ref, r), row_of(kd_ref, r)
            now, spread = [], []
            for f, ref in enumerate(old):
                v, below = row_of(ref, r), row_of(ref, r + 1)
                right = right_of(v, lane)
                side = [kr[t] * (right[t] - v[t]) for t in range(TILES)]
                left = left_of(side, lane)
                down = [kd[t] * (below[t] - v[t]) for t in range(TILES)]
                spread.append([(side[t] - left[t]) + (down[t] - flux[f][t]) for t in range(TILES)])
                flux[f] = down
                now.append(v)
            for t in range(TILES):
                move = EXCHANGE * (now[1][t] - now[0][t])
                new[0][tile_at(r, t), :] = now[0][t] + (spread[0][t] + move)
                new[1][tile_at(r, t), :] = now[1][t] + (TRACER_DIFF * spread[1][t] - move)
        return 0

    lax.fori_loop(0, (count + BATCH - 1) // BATCH, batch, 0)


def clear_outside(row, fields):
    @pl.when(row == 0)
    def _():
        for ref in fields:
            ref[pl.ds((FIRST + 7) * 64, 64), :] = jnp.zeros((64, 128), F32)

    @pl.when(row == ROWS - 1)
    def _():
        for ref in fields:
            ref[pl.ds((FIRST + 16) * 64, 64), :] = jnp.zeros((64, 128), F32)


def clear_margins(fields):
    for ref in fields:
        ref[0:FIRST * 64, :] = jnp.zeros((FIRST * 64, 128), F32)
        ref[(FIRST + 24) * 64:FRAME * 64, :] = jnp.zeros(((FRAME - FIRST - 24) * 64, 128), F32)


def conductivity_kernel(core_ref, k_ref, kf_ref, half_ref, kc_ref):
    to_frame(lambda c: k_ref[:, c], kf_ref, permutation(False))
    half_ref[...] = kf_ref[pl.ds(pl.multiple_of(core_ref[0] * 256, 256), 256), :]
    kc_ref[...] = restrict_sum(sum_rows(kf_ref, 0))


def start_kernel(u_ref, uf_ref, rs_ref):
    order = permutation(False)
    for f in range(2):
        to_frame(lambda c, f=f: u_ref[f, :, c], uf_ref.at[f], order)
        rs_ref[f] = restrict_sum(sum_rows(uf_ref.at[f], 0))


def conductivity_frame(core, k_ref, mine_ref, other_ref, k, kr, kd):
    clear_margins((k,))
    k[(FIRST + HALO) * 64:(FIRST + 2 * HALO) * 64, :] = k_ref[...]
    for part, half in ((mine_ref, core), (other_ref, 1 - core)):
        for side in range(2):
            at = (FIRST + 2 * HALO * side) * 64 + half * 256
            k[pl.ds(pl.multiple_of(at, 64), 256), :] = part[side]
    faces(k, kr, kd)


def steps(one, other, row, kr, kd, low, count, grow):
    def pair(i, _):
        for n, (old, new) in enumerate(((one, other), (other, one))):
            done = 2 * i + n
            sweep(old, new, kr, kd, FIRST + low - grow * done, count + 2 * grow * done)
            clear_outside(row, new)
        return 0

    lax.fori_loop(0, FINE // 2, pair, 0)


def local_kernel(place_ref, own_ref, k_ref, mine_ref, other_ref, rs_ref, kc_ref, out_ref, h, t, h2, t2, k, kr, kd, mix):
    lane = lanes()
    conductivity_frame(place_ref[1], k_ref, mine_ref, other_ref, k, kr, kd)
    for ref in (h, t, h2, t2):
        ref[...] = jnp.zeros_like(ref)
    for f, ref in enumerate((h, t)):
        ref[(FIRST + HALO) * 64:(FIRST + 2 * HALO) * 64, :] = own_ref[f]
    steps((h, t), (h2, t2), place_ref[0], kr, kd, HALO - 1, HALO + 2, 1)
    for b in range(3):
        for f, ref in enumerate((h, t)):
            mix[pl.ds(2 * b + f, 8, stride=8), :] = restrict_sum(sum_rows(ref, FIRST + HALO * b))
    for f in range(2):
        mix[pl.ds(6 + f, 8, stride=8), :] = rs_ref[f]
    kc = kc_ref[...]
    turned = pltpu.roll(kc, 64, 1)
    for j in range(ROWS):
        c, odd = j // 2, j % 2
        d = (c + 1) % CHUNKS if odd else (c - 1) % CHUNKS
        far = mix[8 * d:8 * d + 8, :]
        extra = jnp.concatenate([turned[c:c + 1], kc[c:c + 1], (turned if odd else kc)[d:d + 1], jnp.zeros((5, 128), F32)], axis=0)
        out_ref[j, 0:8, :] = mix[8 * c:8 * c + 8, :]
        out_ref[j, 8:16, :] = jnp.where(lane < 64, far if odd else pltpu.roll(far, 64, 1), extra)


def window_kernel(place_ref, got_ref, w_ref, rf_ref, kc_ref):
    odd = place_ref[2] % 2 == 1
    first = lax.broadcasted_iota(jnp.int32, (16, 128), 0)
    lane = lax.broadcasted_iota(jnp.int32, (16, 128), 1)

    def part(k):
        return got_ref[pl.ds(k, 16, stride=16), :]

    def tiles(full, low, high):
        half = jnp.where(odd, jnp.where(lane < 64, low, 0.0), jnp.where(lane < 64, 0.0, high))
        return jnp.where(odd, full, half), jnp.where(odd, half, full)

    def window(k):
        low = part(8 + k)
        return tiles(part(k), low, pltpu.roll(low, 64, 1))

    high = part(10)
    for s, x in enumerate(tiles(jnp.where(lane < 64, pltpu.roll(part(8), 64, 1), part(9)), pltpu.roll(high, 64, 1), high)):
        kc_ref[16 * s:16 * (s + 1), :] = x
    for f in range(2):
        up, own, down, later = window(f), window(2 + f), window(4 + f), window(6 + f)
        for s in range(2):
            total = own[s] + jnp.where(first == 0, 0.0, pltpu.roll(down[s], 1, 0))
            total = total + jnp.where(first == 15, 0.0, pltpu.roll(up[s], 15, 0))
            at = slice(32 * s + 16 * f, 32 * s + 16 * f + 16)
            rf_ref[at, :] = total
            w = total - later[s]
            for m in range(GROUP):
                w_ref[m, at, :] = w


def field(ref, f):
    return jnp.concatenate([ref[16 * f:16 * f + 16, :], ref[32 + 16 * f:48 + 16 * f, :]], axis=1)


def put(ref, f, x):
    ref[16 * f:16 * f + 16, :] = x[:, :128]
    ref[32 + 16 * f:48 + 16 * f, :] = x[:, 128:]


def coarse_coefficients(kc_ref):
    k = jnp.concatenate([kc_ref[0:16, :], kc_ref[16:32, :]], axis=1)
    width = k.shape[1]
    row = lax.broadcasted_iota(jnp.int32, k.shape, 0)
    scale = 0.5 * (FINE / COARSE) / (COARSEN * COARSEN)
    up = scale * (k + jnp.where(row == 0, 0.0, pltpu.roll(k, 1, 0)))
    down = scale * (k + jnp.where(row == 15, 0.0, pltpu.roll(k, 15, 0)))
    right = scale * (k + pltpu.roll(k, width - 1, 1))
    left = scale * (k + pltpu.roll(k, 1, 1))
    total = up + down + right + left
    keep = 1.0 - EXCHANGE * FINE / COARSE
    return (jnp.where(row == 0, 0.0, up), jnp.where(row == 15, 0.0, down), right, left,
            keep - total, keep - TRACER_DIFF * total)


def coarse_apply(e, coefficients):
    up, down, right, left, mid_h, mid_t = coefficients
    width = up.shape[1]
    trade = EXCHANGE * FINE / COARSE

    def around(v):
        return (up * pltpu.roll(v, 1, 0) + down * pltpu.roll(v, 15, 0)) + (
            right * pltpu.roll(v, width - 1, 1) + left * pltpu.roll(v, 1, 1))

    h, t = e
    for _ in range(COARSE):
        h, t = (around(h) + (mid_h * h + trade * t),
                TRACER_DIFF * around(t) + (mid_t * t + trade * h))
    return h, t


def group_kernel(place_ref, got_ref, kc_ref, sum_ref, own_ref):
    place, group = place_ref[0], place_ref[1]
    coefficients = coarse_coefficients(kc_ref)
    shape = coefficients[0].shape
    zero = jnp.zeros(shape, F32)
    put(own_ref, 0, zero)
    put(own_ref, 1, zero)

    def link(m, e):
        @pl.when(m == place)
        def _():
            put(own_ref, 0, e[0])
            put(own_ref, 1, e[1])
        nxt = coarse_apply(e, coefficients)
        w = got_ref.at[m]
        return nxt[0] + field(w, 0), nxt[1] + field(w, 1)

    e = lax.fori_loop(0, GROUP, link, (zero, zero))
    ahead = [e]
    for _ in range(ZL - 2):
        ahead.append(lax.fori_loop(0, GROUP, lambda _, x: coarse_apply(x, coefficients), ahead[-1]))
    for g in range(ZL):
        for f in range(2):
            x = zero
            for gap in range(1, ZL):
                x = jnp.where(g - group == gap, ahead[gap - 1][f], x)
            put(sum_ref.at[g], f, x)


def close_kernel(place_ref, got_ref, kc_ref, own_ref, rf_ref, out_ref):
    place, group, block = place_ref[0], place_ref[1], place_ref[2]
    coefficients = coarse_coefficients(kc_ref)
    e = tuple(sum(field(got_ref.at[g], f) for g in range(ZL)) for f in range(2))
    e = lax.fori_loop(0, jnp.where(group == 0, 0, place), lambda _, x: coarse_apply(x, coefficients), e)
    e = coarse_apply((e[0] + field(own_ref, 0), e[1] + field(own_ref, 1)), coefficients)
    h, t = e[0] + field(rf_ref, 0), e[1] + field(rf_ref, 1)
    odd = block % 2 == 1
    lane = lax.broadcasted_iota(jnp.int32, (16, 128), 1)
    middle = [jnp.where(odd, pltpu.roll(x[:, :128], 64, 1), x[:, 128:]) for x in (h, t)]
    both = jnp.where(lane < 64, middle[0], pltpu.roll(middle[1], 64, 1))
    for j in range(ROWS):
        out_ref[j] = both


def fine_kernel(place_ref, own_ref, above_ref, below_ref, k_ref, mine_ref, other_ref, ends_ref, mean_ref, h, t, h2, t2, k, kr, kd):
    conductivity_frame(place_ref[1], k_ref, mine_ref, other_ref, k, kr, kd)
    clear_margins((h, t, h2, t2))
    for f, ref in enumerate((h, t)):
        for n, part in enumerate((above_ref, own_ref, below_ref)):
            at = (FIRST + n * HALO) * 64
            ref[at:at + HALO * 64, :] = part[f]
    steps((h, t), (h2, t2), place_ref[0], kr, kd, 1, 3 * HALO - 2, -1)
    back = permutation(True)
    for f, ref in enumerate((h, t)):
        mean_ref[f] = restrict_sum(sum_rows(ref, FIRST + HALO))
        x = jnp.concatenate([
            jnp.concatenate([ref[pl.ds((FIRST + HALO) * 64 + s * 8 + c, 8, stride=64), :] for s in range(TILES)], axis=1)
            for c in range(CHUNKS)], axis=0)
        x = permuted(x, back)
        for c in range(CHUNKS):
            ends_ref[f, :, c * WIDE:(c + 1) * WIDE] = x[8 * c:8 * c + 8, :]


def finish_kernel(place_ref, fine_ref, mean_ref, got_ref, ends_ref, next_ref):
    lane = lanes()
    row = place_ref[0]
    wide = lax.broadcasted_iota(jnp.int32, (16, 128), 1)
    for q in range(CHUNKS):
        even, odd = got_ref[32 * q:32 * q + 16, :], got_ref[32 * q + 16:32 * q + 32, :]
        cols = slice(128 * q, 128 * (q + 1))
        next_ref[0, :, cols] = jnp.where(wide < 64, even, pltpu.roll(odd, 64, 1))
        next_ref[1, :, cols] = jnp.where(wide < 64, pltpu.roll(even, 64, 1), odd)
    even = got_ref[pl.ds(row, 8, stride=32), :]
    odd = got_ref[pl.ds(row + 16, 8, stride=32), :]
    mine = (jnp.where(lane < 64, even, pltpu.roll(odd, 64, 1)), jnp.where(lane < 64, pltpu.roll(even, 64, 1), odd))
    for f in range(2):
        change = mine[f] - mean_ref[f]
        for t in range(TILES):
            spread = jnp.take_along_axis(change, 16 * t + lane // 8, axis=1)
            for c in range(CHUNKS):
                cols = slice(c * WIDE + 128 * t, c * WIDE + 128 * (t + 1))
                ends_ref[f, :, cols] = fine_ref[f, :, cols] + jnp.broadcast_to(spread[c:c + 1], (8, 128))


def call(kernel, outs, scratch, args, scalars=0, name=None, us=1):
    vmem = pl.BlockSpec(memory_space=pltpu.VMEM)
    specs = [pl.BlockSpec(memory_space=pltpu.SMEM)] * scalars + [vmem] * (len(args) - scalars)
    shapes = [jax.ShapeDtypeStruct(s, F32) for s in outs]
    single = len(outs) == 1
    return pl.pallas_call(
        kernel,
        out_shape=shapes[0] if single else shapes,
        in_specs=specs,
        out_specs=vmem if single else [vmem] * len(outs),
        scratch_shapes=[pltpu.VMEM(s, F32) for s in scratch],
        compiler_params=pltpu.CompilerParams(vmem_limit_bytes=VMEM_LIMIT),
        name=name,
        cost_estimate=pl.CostEstimate(flops=0, bytes_accessed=us * 3690000, transcendentals=0),
    )(*args)


def body(starts, conductivity):
    rows_axes, tm_axes = ("y", "z_hi"), ("z_lo", "x", "core")
    u = starts[0]
    row = lax.axis_index(rows_axes).astype(jnp.int32)
    group = lax.axis_index("z_lo").astype(jnp.int32)
    place = lax.axis_index(("x", "core")).astype(jnp.int32)
    core = lax.axis_index("core").astype(jnp.int32)
    here = jnp.stack([row, core])
    places = jnp.stack([place, group, row])

    def from_above(x):
        return lax.ppermute(x, rows_axes, [(i, i + 1) for i in range(ROWS - 1)])

    def from_below(x):
        return lax.ppermute(x, rows_axes, [(i + 1, i) for i in range(ROWS - 1)])

    kf, half, kc = call(conductivity_kernel, [(512, 128), (256, 128), (8, 128)], [], (core[None], conductivity), 1,
                        name="frame_conductivity", us=2)
    k_up, k_down = from_above(half), from_below(half)
    uf, rs = call(start_kernel, [(2, 512, 128), (2, 8, 128)], [], (u,), name="frame_starts", us=3)
    above, below = from_above(uf), from_below(uf)
    slices = ZL * GROUP
    rs_next = lax.ppermute(rs, tm_axes, [(i + 1, i) for i in range(slices - 1)])
    rs_next, k_up, k_down = lax.optimization_barrier((rs_next, k_up, k_down))
    mine = jnp.stack([k_up, k_down])
    other = lax.ppermute(mine, "core", [(0, 1), (1, 0)])
    frame = (FRAME * 64, 128)

    parts = call(local_kernel, [(ROWS, 16, 128)], [frame] * 7 + [(64, 128)],
                 (here, uf, kf, mine, other, rs_next, kc), 1, name="own_contributions", us=7)
    parts = lax.all_to_all(parts, rows_axes, 0, 0)
    parts = parts.reshape(ROWS * 16, 128)
    zero = row // 1024

    def chain(state):
        turn = state[0]
        where = places + turn * zero
        w, rf, kcw = call(window_kernel, [(GROUP, 64, 128), (64, 128), (32, 128)], [], (where, parts), 1, name="windows")
        w = lax.all_to_all(w, ("x", "core"), 0, 0)
        sums, own = call(group_kernel, [(ZL, 64, 128), (64, 128)], [], (where, w, kcw), 1, name="chain_in_group", us=3)
        sums = lax.all_to_all(sums, "z_lo", 0, 0)
        return turn + 1, call(close_kernel, [(ROWS, 16, 128)], [], (where, sums, kcw, own, rf), 1, name="chain_over_groups", us=4)

    _, after = lax.while_loop(lambda state: state[0] < 1 + zero, chain, (jnp.int32(0), jnp.zeros((ROWS, 16, 128), F32)))
    after = lax.all_to_all(after, rows_axes, 0, 0)
    fine, mean = call(fine_kernel, [(2, HALO, NY), (2, 8, 128)], [frame] * 7,
                      (here, uf, above, below, kf, mine, other), 1, name="fine_steps", us=9)
    ends, following = call(finish_kernel, [(2, HALO, NY), (2, ROWS, NY // COARSEN)], [],
                           (here, fine, mean, after.reshape(ROWS * 16, 128)), 1, name="ends", us=2)
    return ends[None], following[None]


def solution(mesh):
    fine_mesh = Mesh(mesh.devices.reshape(ZL, XC, CORE, 4, 4), ("z_lo", "x", "core", "y", "z_hi"))
    tm, rows = ("z_lo", "x", "core"), ("y", "z_hi")
    in_specs = (P(tm, None, rows, None), P(rows, None))
    out_specs = (P(tm, None, rows, None), P(tm, None, None, None))
    return jax.shard_map(body, mesh=fine_mesh, in_specs=in_specs, out_specs=out_specs, check_vma=False)
```
